256 devices in a mesh: slot: 4 (over z_hi, core), seq: 64 (over x, y, z_lo).
Axes of the slice: x: 4, y: 4, z: 8 (z_hi: 2, z_lo: 4; z = z_hi * 4 + z_lo), core: 2. Of those that a mesh axis runs over, the one named last changes fastest.
Arguments:
- queries: bfloat16 [4, 2048, 4096], P('slot', 'seq'), may hold values from -100 to 100
- keys: bfloat16 [4, 2048, 4096], P('slot', 'seq'), may hold values from -6 to 6
- values: bfloat16 [4, 2048, 4096], P('slot', 'seq'), may hold values from -6 to 6
- cache_keys: bfloat16 [4, 2048, 4096], P(None, 'seq'), may hold values from -6 to 6
- cache_values: bfloat16 [4, 2048, 4096], P(None, 'seq'), may hold values from -6 to 6
- span_rank: int32 [4], replicated, may hold values from 0 to 3, each once
- noise_level: int32 [4], replicated, may hold values from 0 to 15
- cache_seen: int32 [4], replicated, may hold values from 0 to 4
- gate_table: float32 [16, 32], replicated, may hold values from 0.25 to 2
Outputs:
- shifted: bfloat16 [4, 2048, 4096], P('slot', 'seq')
The draws below stay inside these ranges and needn't reach their ends.
All inputs are finite; a program needn't handle non-finite values.
Results may differ from the reference program's by a relative error of at most 0.0047.
Values may be sent and summed in bfloat16 or wider, within the bound.
A program may use at most 64 MiB of HBM per device.

```python
import math
import jax
import jax.numpy as jnp
from jax import lax

HEADS = 32
HD = 128
CACHE = 4
LEVELS = 16
TOKENS = 2048
N_SLOT = 4


def shared_base(key):
    return jnp.clip(jax.random.normal(key, (N_SLOT, TOKENS, HEADS * HD), jnp.float32), -6.0, 6.0)


def draw_keys(key, part):
    return shared_base(key).astype(jnp.bfloat16)


def draw_queries(key, part):
    own_key = jax.random.fold_in(key, 3)
    drawn = jnp.clip(jax.random.normal(own_key, (N_SLOT, TOKENS, HEADS * HD), jnp.float32), -6.0, 6.0)
    return drawn.astype(jnp.bfloat16)


def set_ends(result, key, least, top_value):
    dims = result.shape
    index_at = [jax.random.randint(jax.random.fold_in(key, axis), (), 0, dims[axis]) for axis in range(len(dims))]
    result = result.at[tuple(index_at)].set(least)
    longest = dims.index(max(dims))
    index_at[longest] = (index_at[longest] + 1) % dims[longest]
    return result.at[tuple(index_at)].set(top_value)


def level_of(stream_key, dims, pieces, least, top_value):
    level, own = 1.0, jax.random.fold_in(stream_key, 6)
    for position, shards_of in pieces:
        draws = jnp.exp(jax.random.uniform(jax.random.fold_in(own, position), (shards_of,), jnp.float32, least / len(pieces), top_value / len(pieces)))
        level = level * jnp.repeat(draws, dims[position] // shards_of).reshape([-1 if axis == position else 1 for axis in range(len(dims))])
    return level


def scatter_about(key, shape, spread, most, split=(), kind=jnp.bfloat16):
    entries = spread * jax.random.normal(key, shape, jnp.float32)
    if split:
        entries = entries * level_of(key, shape, split, -0.22, 0.18)
    return jnp.clip(entries, -most, most).astype(kind)


def setup_inputs(seed: int = 0) -> dict:
    arg_keys = jax.random.split(jax.random.key(seed), 10)
    return {
        "queries": draw_queries(jax.random.fold_in(arg_keys[9], 71), 0),
        "keys": draw_keys(jax.random.fold_in(arg_keys[9], 71), 0),
        "values": scatter_about(arg_keys[2], (N_SLOT, TOKENS, HEADS * HD), 1.0, 6.0, ((0, 4), (1, 64))),
        "cache_keys": scatter_about(arg_keys[3], (CACHE, TOKENS, HEADS * HD), 1.0, 6.0, ((1, 64),)),
        "cache_values": scatter_about(arg_keys[4], (CACHE, TOKENS, HEADS * HD), 1.0, 6.0, ((1, 64),)),
        "span_rank": jax.random.permutation(arg_keys[5], N_SLOT).astype(jnp.int32),
        "noise_level": set_ends(jax.random.randint(arg_keys[6], (N_SLOT,), 0, LEVELS), jax.random.fold_in(arg_keys[6], 1), 0, LEVELS - 1).astype(jnp.int32),
        "cache_seen": set_ends(jax.random.randint(arg_keys[7], (N_SLOT,), 0, CACHE + 1), jax.random.fold_in(arg_keys[7], 1), 0, CACHE).astype(jnp.int32),
        "gate_table": jnp.clip(jax.random.uniform(arg_keys[8], (LEVELS, HEADS), jnp.float32, 0.25, 2.0), 0.25, 2.0),
    }


NEG_FILL = -1e+30

def block_terms(query_head, key_head, value_head, scale_factor):
    scores = jnp.dot(query_head, key_head.T, preferred_element_type=jnp.float32) * scale_factor
    block_max = lax.optimization_barrier(jnp.max(scores, axis=-1))
    weights = jnp.exp(scores - block_max[:, None])
    block_sum = lax.optimization_barrier(jnp.sum(weights, axis=-1))
    numerator = jnp.dot(weights.astype(jnp.bfloat16), value_head, preferred_element_type=jnp.float32)
    return (numerator, block_max, block_sum)

def reference(queries, keys, values, cache_keys, cache_values, span_rank, noise_level, cache_seen, gate_table):
    head_dim = queries.shape[-1] // HEADS
    scale_factor = 1.0 / math.sqrt(head_dim)
    block_count = N_SLOT + CACHE
    key_blocks = jnp.concatenate([keys, cache_keys], 0)
    value_blocks = jnp.concatenate([values, cache_values], 0)
    key_split = key_blocks.reshape(block_count, TOKENS, HEADS, head_dim).transpose(2, 0, 1, 3)
    value_split = value_blocks.reshape(block_count, TOKENS, HEADS, head_dim).transpose(2, 0, 1, 3)
    results = []
    for slot_idx in range(N_SLOT):
        visible = jnp.concatenate([span_rank <= span_rank[slot_idx], jnp.arange(CACHE) < cache_seen[slot_idx]])
        query_slot = queries[slot_idx].reshape(TOKENS, HEADS, head_dim).transpose(1, 0, 2)
        gates = gate_table[noise_level[slot_idx]]

        def per_head(items):
            query_head, key_all, value_all, gate_value = items
            terms = [block_terms(query_head, key_all[blk], value_all[blk], scale_factor) for blk in range(block_count)]
            numerators = jnp.stack([item[0] for item in terms])
            maxima = jnp.stack([item[1] for item in terms])
            sums_all = jnp.stack([item[2] for item in terms])
            shown = visible[:, None]
            top = lax.optimization_barrier(jnp.max(jnp.where(shown, maxima, NEG_FILL), axis=0))
            coef = jnp.where(shown, jnp.exp(jnp.where(shown, maxima - top[None], 0.0)), 0.0)
            total = lax.optimization_barrier(jnp.sum(coef[:, :, None] * numerators, 0)) / lax.optimization_barrier(jnp.sum(coef * sums_all, 0))[:, None]
            return (gate_value * total).astype(jnp.bfloat16)
        mixed = lax.map(per_head, (query_slot, key_split, value_split, gates))
        results.append(mixed.transpose(1, 0, 2).reshape(TOKENS, HEADS * head_dim))
    attended = jnp.stack(results)
    return jnp.roll(attended, 1, axis=0)
```

```python
import functools
import math

import jax
import jax.numpy as jnp
from jax import lax
from jax.experimental import pallas as pl
from jax.experimental.pallas import tpu as pltpu
from jax.sharding import PartitionSpec as P

HEADS = 32
HD = 128
ROWS = 32
NX, NY, NZ = 4, 4, 8
MESH = pl.DeviceIdType.MESH
BF = jnp.bfloat16
NEG = -1e30


def place():
    slot, seq = lax.axis_index("slot"), lax.axis_index("seq")
    return seq // 16, (seq // 4) % 4, (slot // 2) * 4 + seq % 4, slot % 2


def device(x, y, z, core):
    return ((z // 4) * 2 + core, x * 16 + y * 4 + z % 4)


def wait_bytes(ref, sem):
    pltpu.make_async_copy(ref, ref, sem).wait()


def greet(peers):
    barrier = pltpu.get_barrier_semaphore()
    for peer in peers:
        pl.semaphore_signal(barrier, inc=1, device_id=peer, device_id_type=MESH)
    pl.semaphore_wait(barrier, len(peers))


def remote(src, dst, send, recv, peer):
    pltpu.make_async_remote_copy(
        src_ref=src, dst_ref=dst, send_sem=send, recv_sem=recv, device_id=peer, device_id_type=MESH
    ).start()


def gather_kernel(
    q_ref, k_ref, v_ref, ck_ref, cv_ref, qb, kb, vb,
    sq, sk, sv, sck, scv,
    y_send, y_recv, z_send, z_recv, x_send, x_recv, s_send, s_recv,
):
    x, y, z, c = place()
    zl, zhi = z % 4, z // 4
    odd = z % 2
    q_core = c + odd - 2 * c * odd
    step = 1 - 2 * c
    ahead = device((x + step + NX) % NX, y, z, c)
    behind = device((x - step + NX) % NX, y, z, c)
    other = device(x, y, z, 1 - c)

    peers = [device(x, (y + d) % NY, z, c) for d in range(1, NY)]
    peers += [device(x, y, (z + d) % NZ, c) for d in range(1, NZ)]
    peers += [device(x, y, (z + d) % NZ, 1 - c) for d in range(NZ)]
    peers += [ahead, behind]
    greet(peers)

    pairs = [((z // 2 + e - c + 4) % 4) for e in range(2)]

    def y_cached(ref, held, n):
        for d in (1, 2, 3, 0):
            to = (y + d) % NY
            for e in range(2):
                src = ref.at[pl.ds(2 * c, 2), :, pl.ds(pl.multiple_of(to * 1024 + pairs[e] * 256, 256), 256)]
                dst = held.at[e, :, y]
                if d:
                    remote(src, dst, y_send.at[n], y_recv.at[n], device(x, to, z, c))
                else:
                    pltpu.make_async_copy(src, dst, y_recv.at[n]).start()

    def y_own(ref, held, n):
        for d in (1, 2, 3, 0):
            to = (y + d) % NY
            src = ref.at[0, :, pl.ds(pl.multiple_of(to * 1024, 1024), 1024)]
            dst = held.at[y]
            if d:
                remote(src, dst, y_send.at[n], y_recv.at[n], device(x, to, z, c))
            else:
                pltpu.make_async_copy(src, dst, y_recv.at[n]).start()

    def z_cached(held, out, n):
        wait_bytes(held, y_recv.at[n])
        for e in range(2):
            for w in range(2):
                to = pairs[e] * 2 + w
                src = held.at[e, :, :, :, pl.ds(w * 128, 128)]
                dst = out.at[0, 0, pl.ds(2, 2), zl]

                @pl.when(to == z)
                def _():
                    pltpu.make_async_copy(src, dst, z_recv.at[n]).start()

                @pl.when(to != z)
                def _():
                    remote(src, dst, z_send.at[n], z_recv.at[n], device(x, y, to, c))

    def z_own(held, out, n):
        wait_bytes(held, y_recv.at[n])
        for d in (4, 3, 5, 2, 6, 1, 7, 0):
            to = (z + d) % NZ
            src = held.at[:, :, pl.ds(pl.multiple_of(to * 128, 128), 128)]
            dst = out.at[0, 0, zhi, zl]
            if d:
                remote(src, dst, z_send.at[n], z_recv.at[n], device(x, y, to, c))
            else:
                pltpu.make_async_copy(src, dst, z_recv.at[n]).start()

    def z_query(n):
        wait_bytes(sq, y_recv.at[n])
        dst = qb.at[zhi * 2 + c, zl // 2]
        for d in (4, 3, 5, 2, 6, 1, 7, 0):
            to = (z + d) % NZ
            src = sq.at[:, :, pl.ds(pl.multiple_of(to * 128, 128), 128)]
            if d:
                remote(src, dst, z_send.at[n], z_recv.at[n], device(x, y, to, q_core))
            else:

                @pl.when(odd == 0)
                def _():
                    pltpu.make_async_copy(src, dst, z_recv.at[n]).start()

                @pl.when(odd == 1)
                def _():
                    remote(src, dst, z_send.at[n], z_recv.at[n], other)

    def unit(out, n, j, owner=0):
        return out.at[owner, j, pl.ds(2, 2) if n < 2 else pl.ds(0, 2)]

    def share(out, n, j):
        remote(unit(out, n, j), unit(out, n, j, 1), s_send.at[n, j], s_recv.at[n, j], other)

    def x0(out, n):
        wait_bytes(unit(out, n, 0), z_recv.at[n])
        remote(unit(out, n, 0), unit(out, n, 1), x_send.at[n, 0], x_recv.at[n, 0], ahead)
        remote(unit(out, n, 0), unit(out, n, 3), x_send.at[n, 1], x_recv.at[n, 1], behind)
        share(out, n, 0)

    def x1(out, n):
        wait_bytes(unit(out, n, 1), x_recv.at[n, 0])
        remote(unit(out, n, 1), unit(out, n, 2), x_send.at[n, 2], x_recv.at[n, 2], ahead)
        share(out, n, 1)
        wait_bytes(unit(out, n, 3), x_recv.at[n, 1])
        share(out, n, 3)

    def x2(out, n):
        wait_bytes(unit(out, n, 2), x_recv.at[n, 2])
        share(out, n, 2)

    CK, CV, K, V, Q = range(5)
    y_cached(ck_ref, sck, CK)
    y_cached(cv_ref, scv, CV)
    y_own(q_ref, sq, Q)
    y_own(k_ref, sk, K)
    y_own(v_ref, sv, V)
    z_cached(sck, kb, CK)
    z_cached(scv, vb, CV)
    z_query(Q)
    x0(kb, CK)
    z_own(sk, kb, K)
    x0(vb, CV)
    z_own(sv, vb, V)
    x1(kb, CK)
    x0(kb, K)
    x1(vb, CV)
    x2(kb, CK)
    x0(vb, V)
    x2(vb, CV)
    x1(kb, K)
    x1(vb, V)
    x2(kb, K)
    x2(vb, V)

    wait_bytes(sq, z_recv.at[Q])
    for n, out in ((CK, kb), (CV, vb), (K, kb), (V, vb)):
        for j in range(4):
            wait_bytes(unit(out, n, j, 1), s_recv.at[n, j])
            wait_bytes(unit(out, n, j), s_send.at[n, j])
        for j in range(3):
            wait_bytes(unit(out, n, j), x_send.at[n, j])
    for n, held in ((Q, sq), (K, sk), (V, sv)):
        wait_bytes(held.at[pl.ds(0, 3)], y_send.at[n])
    for n, held in ((CK, sck), (CV, scv)):
        wait_bytes(held.at[:, :, pl.ds(0, 3)], y_send.at[n])
        wait_bytes(held.at[:, :, pl.ds(0, 3)], z_send.at[n])
    for n, held in ((K, sk), (V, sv)):
        wait_bytes(held.at[:, :, pl.ds(0, 896)], z_send.at[n])

    @pl.when(odd == 0)
    def _():
        wait_bytes(sq.at[:, :, pl.ds(0, 896)], z_send.at[Q])

    @pl.when(odd == 1)
    def _():
        wait_bytes(sq, z_send.at[Q])


def gather(q, k, v, ck, cv):
    dma = pltpu.SemaphoreType.DMA
    return pl.pallas_call(
        gather_kernel,
        out_shape=(
            jax.ShapeDtypeStruct((4, 2, NY, ROWS, HD), BF),
            jax.ShapeDtypeStruct((2, NX, 4, 4, NY, ROWS, HD), BF),
            jax.ShapeDtypeStruct((2, NX, 4, 4, NY, ROWS, HD), BF),
        ),
        in_specs=[pl.BlockSpec(memory_space=pl.ANY)] * 5,
        out_specs=[pl.BlockSpec(memory_space=pl.ANY)] * 3,
        scratch_shapes=[
            pltpu.VMEM((NY, ROWS, 1024), BF),
            pltpu.VMEM((NY, ROWS, 1024), BF),
            pltpu.VMEM((NY, ROWS, 1024), BF),
            pltpu.VMEM((2, 2, NY, ROWS, 256), BF),
            pltpu.VMEM((2, 2, NY, ROWS, 256), BF),
            dma((5,)), dma((5,)), dma((5,)), dma((5,)),
            dma((4, 3)), dma((4, 3)), dma((4, 4)), dma((4, 4)),
        ],
        compiler_params=pltpu.CompilerParams(
            collective_id=0, has_side_effects=True, vmem_limit_bytes=16 * 2**20
        ),
        name="gather",
    )(q, k, v, ck, cv)


def attend_kernel(rank, level, seen, where, gate, q_ref, k_ref, v_ref, o_ref, acc, top, den):
    blk = pl.program_id(0)
    core, head = where[0], where[1]
    owner, i = blk // 4, blk % 4
    holder = jnp.where(owner == 0, core, 1 - core)
    scale = math.log2(math.e) / math.sqrt(HD)

    @pl.when(blk == 0)
    def _():
        acc[...] = jnp.zeros_like(acc)
        den[...] = jnp.zeros_like(den)
        top[...] = jnp.full_like(top, NEG)

    for s in range(4):
        in_flight = rank[jnp.where(i < 2, 2 * i + holder, 0)] <= rank[s]
        cached = 2 * holder + i - 2 < seen[s]
        visible = jnp.where(i < 2, in_flight, cached)

        @pl.when(visible)
        def _():
            scores = lax.dot_general(
                q_ref[s], k_ref[0, :, 0].reshape(2048, HD), (((1,), (1,)), ((), ())),
                preferred_element_type=jnp.float32,
            )
            old = top[s, :, :1]
            new = jnp.maximum(old, jnp.max(scores, axis=1, keepdims=True))
            weights = jnp.exp2(scores * scale - new * scale)
            fade = jnp.exp2((old - new) * scale)
            den[s] = den[s] * fade + jnp.sum(weights, axis=1, keepdims=True)
            acc[s] = acc[s] * fade + jnp.dot(
                weights.astype(BF), v_ref[0, :, 0].reshape(2048, HD),
                preferred_element_type=jnp.float32,
            )
            top[s] = jnp.broadcast_to(new, top.shape[1:])

    @pl.when(blk == 7)
    def _():
        for s in range(4):
            o_ref[s] = (gate[level[s], head] * (acc[s] / den[s])).astype(BF)


def attend(rank, level, seen, where, gate, q, k, v):
    smem = pl.BlockSpec(memory_space=pltpu.SMEM)
    block = pl.BlockSpec((1, NX, 1, 512, HD), lambda b: (b // 4, 0, b % 4, 0, 0))
    whole = pl.BlockSpec((4, 256, HD), lambda b: (0, 0, 0))
    return pl.pallas_call(
        attend_kernel,
        grid=(8,),
        out_shape=jax.ShapeDtypeStruct((4, 256, HD), BF),
        in_specs=[smem] * 5 + [whole, block, block],
        out_specs=whole,
        scratch_shapes=[
            pltpu.VMEM((4, 256, HD), jnp.float32),
            pltpu.VMEM((4, 256, HD), jnp.float32),
            pltpu.VMEM((4, 256, HD), jnp.float32),
        ],
        compiler_params=pltpu.CompilerParams(vmem_limit_bytes=40 * 2**20),
        name="attend",
    )(rank, level, seen, where, gate, q, k, v)


def return_kernel(a_ref, o_ref, held, y_send, y_recv, z_send, z_recv):
    x, y, z, c = place()
    peers = [device(x, (y + d) % NY, z, c) for d in range(1, NY)]
    peers += [device(x, y, (z + d) % NZ, c) for d in range(1, NZ)]
    peers += [device(x, y, (z + d) % NZ, 1 - c) for d in range(NZ)]
    greet(peers)

    for d in (4, 3, 5, 2, 6, 1, 7, 0):
        to = (z + d) % NZ
        odd = to % 2
        core = 1 - (c + odd - 2 * c * odd)
        span = (2 * (to // 4) + core + 3) % 4
        src = a_ref.at[span, (to % 4) // 2]
        dst = held.at[:, :, pl.ds(pl.multiple_of(z * 128, 128), 128)]
        if d:
            remote(src, dst, z_send, z_recv, device(x, y, to, core))
        else:

            @pl.when(odd == 1)
            def _():
                pltpu.make_async_copy(src, dst, z_recv).start()

            @pl.when(odd == 0)
            def _():
                remote(src, dst, z_send, z_recv, device(x, y, z, 1 - c))

    wait_bytes(held, z_recv)
    for d in (2, 1, 3, 0):
        to = (y + d) % NY
        src = held.at[to]
        dst = o_ref.at[0, :, pl.ds(pl.multiple_of(y * 1024, 1024), 1024)]
        if d:
            remote(src, dst, y_send, y_recv, device(x, to, z, c))
        else:
            pltpu.make_async_copy(src, dst, y_recv).start()
    wait_bytes(o_ref, y_recv)
    wait_bytes(held.at[pl.ds(0, 3)], y_send)

    @pl.when(z % 2 == 1)
    def _():
        wait_bytes(held.at[:, :, pl.ds(0, 896)], z_send)

    @pl.when(z % 2 == 0)
    def _():
        wait_bytes(held, z_send)


def send_back(a):
    dma = pltpu.SemaphoreType.DMA
    return pl.pallas_call(
        return_kernel,
        out_shape=jax.ShapeDtypeStruct((1, ROWS, HEADS * HD), BF),
        in_specs=[pl.BlockSpec(memory_space=pl.ANY)],
        out_specs=pl.BlockSpec(memory_space=pl.ANY),
        scratch_shapes=[pltpu.VMEM((NY, ROWS, 1024), BF), dma, dma, dma, dma],
        compiler_params=pltpu.CompilerParams(
            collective_id=1, has_side_effects=True, vmem_limit_bytes=16 * 2**20
        ),
        name="send_back",
    )(a)


def local(q, k, v, ck, cv, rank, level, seen, gate):
    qb, kb, vb = gather(q, k, v, ck, cv)
    _, y, z, c = place()
    where = jnp.stack([c, y * NZ + z]).astype(jnp.int32)
    mixed = attend(
        rank, level, seen, where, gate,
        qb.reshape(4, 256, HD), kb.reshape(2, NX, 4, 512, HD), vb.reshape(2, NX, 4, 512, HD),
    )
    return send_back(mixed.reshape(4, 2, NY, ROWS, HD))


def solution(mesh):
    own, cached = P("slot", "seq", None), P(None, "seq", None)
    placed = (own, own, own, cached, cached, P(), P(), P(), P())
    return jax.shard_map(local, mesh=mesh, in_specs=placed, out_specs=own, check_vma=False)
```

```python
import math

import jax
import jax.numpy as jnp
from jax import lax
from jax.experimental import pallas as pl
from jax.experimental.pallas import tpu as pltpu
from jax.sharding import PartitionSpec as P

HEADS = 32
HD = 128
ROWS = 32
NX, NY, NZ = 4, 4, 8
MESH = pl.DeviceIdType.MESH
BF = jnp.bfloat16
F32 = jnp.float32
FAR = 1e30
SCALE = math.log2(math.e) / math.sqrt(HD)

CK, CV, K, V, Q = range(5)

BEFORE = "y0 y1 y4 y2 y3 z0 z1 a0 z4 a1 z2 z3 q"
DURING = [
    "s00",
    "s10 b0",
    "b1 s01",
    "s11 d0 a2",
    "d1 s02",
    "s12 c0 a3",
    "c1 s03",
    "s13 b2",
    "b3 s20",
    "s30 d2",
    "d3 s21",
    "s31",
    "s22",
    "s32 c2",
    "c3 s23",
    "s33",
]


def place():
    slot, seq = lax.axis_index("slot"), lax.axis_index("seq")
    return seq // 16, (seq // 4) % 4, (slot // 2) * 4 + seq % 4, slot % 2


def device(x, y, z, core):
    return ((z // 4) * 2 + core, x * 16 + y * 4 + z % 4)


def wait_bytes(ref, sem):
    pltpu.make_async_copy(ref, ref, sem).wait()


def greet(peers):
    barrier = pltpu.get_barrier_semaphore()
    for peer in peers:
        pl.semaphore_signal(barrier, inc=1, device_id=peer, device_id_type=MESH)
    pl.semaphore_wait(barrier, len(peers))


def remote(src, dst, send, recv, peer):
    pltpu.make_async_remote_copy(
        src_ref=src, dst_ref=dst, send_sem=send, recv_sem=recv, device_id=peer, device_id_type=MESH
    ).start()


def local_copy(src, dst, sem):
    pltpu.make_async_copy(src, dst, sem).start()


def kernel(
    q_ref, k_ref, v_ref, ck_ref, cv_ref, rank_ref, level_ref, seen_ref, gate_ref, o_ref,
    rank, level, seen, gate, qb, kb, vb, sq, sk, sv, sck, scv, att, ret,
    scores, peak, acc, top, den,
    scalar_sem, y_send, y_recv, z_send, z_recv, x_send, x_recv, s_send, s_recv,
    back_send, back_recv,
):
    x, y, z, c = place()
    zl, zhi = z % 4, z // 4
    odd = z % 2
    head = y * NZ + z
    q_core = c + odd - 2 * c * odd
    step_x = 1 - 2 * c
    ahead = device((x + step_x + NX) % NX, y, z, c)
    behind = device((x - step_x + NX) % NX, y, z, c)
    other = device(x, y, z, 1 - c)

    small = ((rank_ref, rank), (level_ref, level), (seen_ref, seen), (gate_ref, gate))
    for n, (src, dst) in enumerate(small):
        local_copy(src, dst, scalar_sem.at[n])

    peers = [device(x, (y + d) % NY, z, c) for d in range(1, NY)]
    peers += [device(x, y, (z + d) % NZ, c) for d in range(1, NZ)]
    peers += [device(x, y, (z + d) % NZ, 1 - c) for d in range(NZ)]
    peers += [ahead, behind]
    greet(peers)

    pairs = [((z // 2 + e - c + 4) % 4) for e in range(2)]
    held = {Q: sq, K: sk, V: sv, CK: sck, CV: scv}
    given = {Q: q_ref, K: k_ref, V: v_ref, CK: ck_ref, CV: cv_ref}
    full = {CK: kb, K: kb, CV: vb, V: vb}

    def stage_y(n):
        for d in (1, 2, 3, 0):
            to = (y + d) % NY
            if n in (CK, CV):
                parts = [
                    (
                        given[n].at[
                            pl.ds(2 * c, 2), :,
                            pl.ds(pl.multiple_of(to * 1024 + pairs[e] * 256, 256), 256),
                        ],
                        held[n].at[e, :, y],
                    )
                    for e in range(2)
                ]
            else:
                columns = pl.ds(pl.multiple_of(to * 1024, 1024), 1024)
                parts = [(given[n].at[0, :, columns], held[n].at[y])]
            for src, dst in parts:
                if d:
                    remote(src, dst, y_send.at[n], y_recv.at[n], device(x, to, z, c))
                else:
                    local_copy(src, dst, y_recv.at[n])

    def stage_z(n):
        wait_bytes(held[n], y_recv.at[n])
        if n in (CK, CV):
            for e in range(2):
                for w in range(2):
                    to = pairs[e] * 2 + w
                    src = held[n].at[e, :, :, :, pl.ds(w * 128, 128)]
                    dst = full[n].at[0, 0, pl.ds(2, 2), zl]

                    @pl.when(to == z)
                    def _():
                        local_copy(src, dst, z_recv.at[n])

                    @pl.when(to != z)
                    def _():
                        remote(src, dst, z_send.at[n], z_recv.at[n], device(x, y, to, c))

            return
        for d in (4, 3, 5, 2, 6, 1, 7, 0):
            to = (z + d) % NZ
            src = held[n].at[:, :, pl.ds(pl.multiple_of(to * 128, 128), 128)]
            if n == Q:
                dst, core = qb.at[zhi * 2 + c, zl // 2], q_core
            else:
                dst, core = full[n].at[0, 0, zhi, zl], c
            if d:
                remote(src, dst, z_send.at[n], z_recv.at[n], device(x, y, to, core))
            elif n != Q:
                local_copy(src, dst, z_recv.at[n])
            else:

                @pl.when(odd == 0)
                def _():
                    local_copy(src, dst, z_recv.at[n])

                @pl.when(odd == 1)
                def _():
                    remote(src, dst, z_send.at[n], z_recv.at[n], other)

    def group(n, j, owner=0):
        return full[n].at[owner, j, pl.ds(2 if n in (CK, CV) else 0, 2)]

    def share(n, j):
        remote(group(n, j), group(n, j, 1), s_send.at[n, j], s_recv.at[n, j], other)

    def event(text):
        kind, n = text[0], int(text[1]) if len(text) > 1 else Q
        if kind == "y":
            stage_y(n)
        elif kind == "z":
            stage_z(n)
        elif kind == "q":
            wait_bytes(sq, z_recv.at[Q])
        elif kind == "a":
            wait_bytes(group(n, 0), z_recv.at[n])
            remote(group(n, 0), group(n, 1), x_send.at[n, 0], x_recv.at[n, 0], ahead)
            remote(group(n, 0), group(n, 2), x_send.at[n, 1], x_recv.at[n, 1], behind)
            share(n, 0)
        elif kind == "b":
            wait_bytes(group(n, 1), x_recv.at[n, 0])
            remote(group(n, 1), group(n, 3), x_send.at[n, 2], x_recv.at[n, 2], ahead)
            share(n, 1)
        elif kind == "d":
            wait_bytes(group(n, 2), x_recv.at[n, 1])
            share(n, 2)
        elif kind == "c":
            wait_bytes(group(n, 3), x_recv.at[n, 2])
            share(n, 3)
        else:
            j = int(text[2])
            wait_bytes(group(n, j, 1), s_recv.at[n, j])

    def matmul_scores(n, s, sub):
        keys = kb[n % 2, (n % 8) // 2, 2 * (1 - n // 8) + sub].reshape(512, HD)
        return lax.dot_general(
            keys, qb[s].reshape(256, HD), (((1,), (1,)), ((), ())), preferred_element_type=F32
        )

    def put_scores(buf, n, s, sub):
        tile = matmul_scores(n, s, sub)
        scores[buf, sub] = tile
        peak[buf, sub] = jnp.max(tile.reshape(64, 8, 256), axis=0)

    def step(n, s, after, after_s):
        buf = s % 2
        across = slice(s * 256, (s + 1) * 256)
        owner, in_flight = n % 2, n // 8
        holder = c + owner - 2 * c * owner
        shown = []
        for sub in range(2):
            span = rank[holder + 2 * sub] <= rank[s]
            cached = 2 * holder + sub < seen[s]
            shown.append(jnp.where(in_flight == 1, span.astype(jnp.int32), cached.astype(jnp.int32)) > 0)
        old = top[:, across]
        new = old
        for sub in range(2):
            most = jnp.max(peak[buf, sub], axis=0, keepdims=True) * SCALE
            new = jnp.maximum(new, jnp.where(shown[sub], most, -FAR))
        fade = jnp.exp2(old - new)
        total = jnp.zeros((HD, 256), F32)
        summed = jnp.zeros((8, 256), F32)
        for sub in range(2):
            put_scores(1 - buf, after, after_s, sub)
            shift = jnp.where(shown[sub], new, FAR)
            weights = jnp.exp2(scores[buf, sub] * SCALE - shift)
            summed = summed + jnp.sum(weights.reshape(64, 8, 256), axis=0)
            across_values = vb[owner, (n % 8) // 2, 2 * (1 - in_flight) + sub].reshape(512, HD).T
            total = total + lax.dot_general(
                across_values, weights.astype(BF), (((1,), (0,)), ((), ())),
                preferred_element_type=F32,
            )
        den[:, across] = den[:, across] * fade + summed
        acc[:, across] = acc[:, across] * fade + total
        top[:, across] = new

    for text in BEFORE.split():
        event(text)
    for n, (_, dst) in enumerate(small):
        wait_bytes(dst, scalar_sem.at[n])
    acc[...] = jnp.zeros_like(acc)
    den[...] = jnp.zeros_like(den)
    top[...] = jnp.full_like(top, -FAR)
    for sub in range(2):
        put_scores(0, 0, 0, sub)

    def item(n, carry):
        for m, texts in enumerate(DURING):

            @pl.when(n == m)
            def _():
                for text in texts.split():
                    event(text)

        for s in range(4):
            if s < 3:
                step(n, s, n, s + 1)
            else:
                step(n, s, jnp.minimum(n + 1, 15), 0)
        return carry

    lax.fori_loop(0, 16, item, 0)

    for s in range(4):
        across = slice(s * 256, (s + 1) * 256)
        gain = gate[level[s], head] / jnp.sum(den[:, across], axis=0, keepdims=True)
        att[s] = (acc[:, across] * gain).T.astype(BF).reshape(2, NY, ROWS, HD)
        span = (s + 1) % 4
        parity = (s % 2 + c) % 2
        for half in range(2):
            to = (span // 2) * 4 + 2 * half + parity
            itself = jnp.logical_and(to == z, c == span % 2)
            src = att.at[s, half]
            dst = ret.at[:, :, pl.ds(pl.multiple_of(z * 128, 128), 128)]

            @pl.when(itself)
            def _():
                local_copy(src, dst, back_recv.at[0])

            @pl.when(jnp.logical_not(itself))
            def _():
                remote(src, dst, back_send.at[0], back_recv.at[0], device(x, y, to, span % 2))

    wait_bytes(ret, back_recv.at[0])
    for d in (2, 1, 3, 0):
        to = (y + d) % NY
        src = ret.at[to]
        dst = o_ref.at[0, :, pl.ds(pl.multiple_of(y * 1024, 1024), 1024)]
        if d:
            remote(src, dst, back_send.at[1], back_recv.at[1], device(x, to, z, c))
        else:
            local_copy(src, dst, back_recv.at[1])

    for n in (CK, CV, K, V):
        for j in range(4):
            wait_bytes(group(n, j), s_send.at[n, j])
        for j in range(3):
            wait_bytes(group(n, j), x_send.at[n, j])
    for n in (Q, K, V):
        wait_bytes(held[n].at[pl.ds(0, 3)], y_send.at[n])
    for n in (CK, CV):
        wait_bytes(held[n].at[:, :, pl.ds(0, 3)], y_send.at[n])
        wait_bytes(held[n].at[:, :, pl.ds(0, 3)], z_send.at[n])
    for n in (K, V):
        wait_bytes(held[n].at[:, :, pl.ds(0, 896)], z_send.at[n])

    @pl.when(odd == 0)
    def _():
        wait_bytes(sq.at[:, :, pl.ds(0, 896)], z_send.at[Q])
        wait_bytes(ret, back_send.at[0])

    @pl.when(odd == 1)
    def _():
        wait_bytes(sq, z_send.at[Q])
        wait_bytes(ret.at[:, :, pl.ds(0, 896)], back_send.at[0])

    wait_bytes(ret.at[pl.ds(0, 3)], back_send.at[1])
    wait_bytes(o_ref, back_recv.at[1])


def local(*operands):
    dma = pltpu.SemaphoreType.DMA
    smem, vmem = pltpu.SMEM, pltpu.VMEM
    everything = (2, NX, 4, 4, NY, ROWS, HD)
    work = 4 * 1024 * 16384 * HD
    return pl.pallas_call(
        kernel,
        out_shape=jax.ShapeDtypeStruct((1, ROWS, HEADS * HD), BF),
        in_specs=[pl.BlockSpec(memory_space=pl.ANY)] * 9,
        out_specs=pl.BlockSpec(memory_space=pl.ANY),
        scratch_shapes=[
            smem((4,), jnp.int32), smem((4,), jnp.int32), smem((4,), jnp.int32), smem((16, 32), F32),
            vmem((4, 2, NY, ROWS, HD), BF), vmem(everything, BF), vmem(everything, BF),
            vmem((NY, ROWS, 1024), BF), vmem((NY, ROWS, 1024), BF), vmem((NY, ROWS, 1024), BF),
            vmem((2, 2, NY, ROWS, 256), BF), vmem((2, 2, NY, ROWS, 256), BF),
            vmem((4, 2, NY, ROWS, HD), BF), vmem((NY, ROWS, 1024), BF),
            vmem((2, 2, 512, 256), F32), vmem((2, 2, 8, 256), F32),
            vmem((HD, 1024), F32), vmem((1, 1024), F32), vmem((8, 1024), F32),
            dma((4,)), dma((5,)), dma((5,)), dma((5,)), dma((5,)),
            dma((4, 3)), dma((4, 3)), dma((4, 4)), dma((4, 4)), dma((2,)), dma((2,)),
        ],
        compiler_params=pltpu.CompilerParams(
            collective_id=0, has_side_effects=True, vmem_limit_bytes=56 * 2**20
        ),
        cost_estimate=pl.CostEstimate(
            flops=work, bytes_accessed=16 * 2**20, transcendentals=1024 * 16384
        ),
        name="attend_all",
    )(*operands)


def solution(mesh):
    own, cached = P("slot", "seq", None), P(None, "seq", None)
    placed = (own, own, own, cached, cached, P(), P(), P(), P())
    return jax.shard_map(local, mesh=mesh, in_specs=placed, out_specs=own, check_vma=False)
```

```python
import math

import jax
import jax.numpy as jnp
from jax import lax
from jax.experimental import pallas as pl
from jax.experimental.pallas import tpu as pltpu
from jax.sharding import PartitionSpec as P

HEADS = 32
HD = 128
ROWS = 32
NX, NY, NZ = 4, 4, 8
MESH = pl.DeviceIdType.MESH
BF = jnp.bfloat16
F32 = jnp.float32
FAR = 1e30
SCALE = math.log2(math.e) / math.sqrt(HD)

CK, CV, K, V, Q = range(5)
UNITS = ((CK, 2, 1), (CK, 3, 1), (CV, 2, 2), (K, 0, 2), (V, 0, 2), (Q, 0, 2))
QUERY = 5

BEFORE = ("y0", "y1", "Z0", "Z1", "y2", "y3", "y4", "z0", "z1", "z2", "a0", "Y", "a1", "z3", "a2", "z4", "q")
DURING = (
    ("s00", "s10"),
    ("b0", "b1", "s20"),
    ("b2", "a3", "s01", "s11"),
    ("d0", "d1", "s21"),
    ("d2", "s02", "s12"),
    ("c0", "c1", "a4", "s22"),
    ("c2", "s03", "s13"),
    ("s23",),
    ("s30",),
    ("b3", "s40",),
    ("b4", "s31"),
    ("d3", "s41"),
    ("d4", "s32"),
    ("c3", "s42"),
    ("c4", "s33"),
    ("s43",),
)


def place():
    slot, seq = lax.axis_index("slot"), lax.axis_index("seq")
    return seq // 16, (seq // 4) % 4, (slot // 2) * 4 + seq % 4, slot % 2


def device(x, y, z, core):
    return ((z // 4) * 2 + core, x * 16 + y * 4 + z % 4)


def wait_bytes(ref, sem):
    pltpu.make_async_copy(ref, ref, sem).wait()


def greet(peers):
    barrier = pltpu.get_barrier_semaphore()
    for peer in peers:
        pl.semaphore_signal(barrier, inc=1, device_id=peer, device_id_type=MESH)
    pl.semaphore_wait(barrier, len(peers))


def remote(src, dst, send, recv, peer):
    pltpu.make_async_remote_copy(
        src_ref=src, dst_ref=dst, send_sem=send, recv_sem=recv, device_id=peer, device_id_type=MESH
    ).start()


def local_copy(src, dst, sem):
    pltpu.make_async_copy(src, dst, sem).start()


def kernel(
    q_ref, k_ref, v_ref, ck_ref, cv_ref, rank_ref, level_ref, seen_ref, gate_ref, o_ref,
    rank, level, seen, gate, qb, kb, vb, sq, sk, sv, sck, scv, att, ret,
    scores, peak, acc, top, den,
    scalar_sem, y_send, y_recv, z_send, z_recv, x_send, x_recv, s_send, s_recv,
    back_send, back_recv,
):
    x, y, z, c = place()
    zl, zhi = z % 4, z // 4
    odd = z % 2
    head = y * NZ + z
    q_core = c + odd - 2 * c * odd
    step_x = 1 - 2 * c
    ahead = device((x + step_x + NX) % NX, y, z, c)
    behind = device((x - step_x + NX) % NX, y, z, c)
    other = device(x, y, z, 1 - c)

    small = ((rank_ref, rank), (level_ref, level), (seen_ref, seen), (gate_ref, gate))
    for n, (src, dst) in enumerate(small):
        local_copy(src, dst, scalar_sem.at[n])

    peers = [device(x, (y + d) % NY, z, c) for d in range(1, NY)]
    peers += [device(x, y, (z + d) % NZ, c) for d in range(1, NZ)]
    peers += [device(x, y, (z + d) % NZ, 1 - c) for d in range(NZ)]
    peers += [ahead, behind]
    greet(peers)

    pairs = [((z // 2 + e - c + 4) % 4) for e in range(2)]
    held = {Q: sq, K: sk, V: sv, CK: sck, CV: scv}
    given = {Q: q_ref, K: k_ref, V: v_ref, CK: ck_ref, CV: cv_ref}
    full = {CK: kb, K: kb, CV: vb, V: vb}

    def stage_y(u):
        n, first, count = UNITS[u]
        for d in (1, 2, 3, 0):
            to = (y + d) % NY
            if n in (CK, CV):
                parts = [
                    (
                        given[n].at[
                            pl.ds(2 * c + first - 2, count), :,
                            pl.ds(pl.multiple_of(to * 1024 + pairs[e] * 256, 256), 256),
                        ],
                        held[n].at[e, pl.ds(first - 2, count), y],
                    )
                    for e in range(2)
                ]
            else:
                columns = pl.ds(pl.multiple_of(to * 1024, 1024), 1024)
                parts = [(given[n].at[0, :, columns], held[n].at[y])]
            for src, dst in parts:
                if d:
                    remote(src, dst, y_send.at[u], y_recv.at[u], device(x, to, z, c))
                else:
                    local_copy(src, dst, y_recv.at[u])

    def held_unit(u):
        n, first, count = UNITS[u]
        return held[n].at[:, pl.ds(first - 2, count)] if n in (CK, CV) else held[n]

    def stage_z(u):
        n, first, count = UNITS[u]
        wait_bytes(held_unit(u), y_recv.at[u])
        if n in (CK, CV):
            for e in (0, 1):
                for w in range(2):
                    to = pairs[e] * 2 + w
                    src = held[n].at[e, pl.ds(first - 2, count), :, :, pl.ds(w * 128, 128)]
                    dst = full[n].at[0, 0, pl.ds(first, count), zl]

                    @pl.when(to == z)
                    def _():
                        local_copy(src, dst, z_recv.at[u])

                    @pl.when(to != z)
                    def _():
                        remote(src, dst, z_send.at[u], z_recv.at[u], device(x, y, to, c))

            return
        for d in (4, 3, 5, 2, 6, 1, 7, 0):
            to = (z + d) % NZ
            src = held[n].at[:, :, pl.ds(pl.multiple_of(to * 128, 128), 128)]
            dst = full[n].at[0, 0, zhi, zl]
            if d:
                remote(src, dst, z_send.at[u], z_recv.at[u], device(x, y, to, c))
            else:
                local_copy(src, dst, z_recv.at[u])

    def query_z(part):
        for d in ((4, 3, 5, 2), (6, 1, 7, 0))[part]:
            to = (z + d) % NZ
            for row in range(NY):
                src = q_ref.at[0, :, pl.ds(pl.multiple_of(row * 1024 + to * 128, 128), 128)]
                dst = sq.at[row, zhi * 2 + c, zl // 2]
                if d:
                    remote(src, dst, z_send.at[QUERY], z_recv.at[QUERY], device(x, y, to, q_core))
                else:

                    @pl.when(odd == 0)
                    def _():
                        local_copy(src, dst, z_recv.at[QUERY])

                    @pl.when(odd == 1)
                    def _():
                        remote(src, dst, z_send.at[QUERY], z_recv.at[QUERY], other)

    def query_y():
        wait_bytes(sq, z_recv.at[QUERY])
        for d in (1, 2, 3, 0):
            to = (y + d) % NY
            dst = qb.at[:, :, y]
            if d:
                remote(sq.at[to], dst, y_send.at[QUERY], y_recv.at[QUERY], device(x, to, z, c))
            else:
                local_copy(sq.at[to], dst, y_recv.at[QUERY])

    def group(u, j, owner=0):
        n, first, count = UNITS[u]
        return full[n].at[owner, j, pl.ds(first, count)]

    def share(u, j):
        remote(group(u, j), group(u, j, 1), s_send.at[u, j], s_recv.at[u, j], other)

    def event(text):
        kind = text[0]
        u = int(text[1]) if len(text) > 1 else QUERY
        if kind == "y":
            stage_y(u)
        elif kind == "z":
            stage_z(u)
        elif kind == "Z":
            query_z(u)
        elif kind == "Y":
            query_y()
        elif kind == "q":
            wait_bytes(qb, y_recv.at[QUERY])
        elif kind == "a":
            wait_bytes(group(u, 0), z_recv.at[u])
            remote(group(u, 0), group(u, 1), x_send.at[u, 0], x_recv.at[u, 0], ahead)
            remote(group(u, 0), group(u, 2), x_send.at[u, 1], x_recv.at[u, 1], behind)
            share(u, 0)
        elif kind == "b":
            wait_bytes(group(u, 1), x_recv.at[u, 0])
            remote(group(u, 1), group(u, 3), x_send.at[u, 2], x_recv.at[u, 2], ahead)
            share(u, 1)
        elif kind == "d":
            wait_bytes(group(u, 2), x_recv.at[u, 1])
            share(u, 2)
        elif kind == "c":
            wait_bytes(group(u, 3), x_recv.at[u, 2])
            share(u, 3)
        else:
            j = int(text[2])
            wait_bytes(group(u, j, 1), s_recv.at[u, j])

    def matmul_scores(n, s, sub):
        keys = kb[n % 2, (n % 8) // 2, 2 * (1 - n // 8) + sub].reshape(512, HD)
        return lax.dot_general(
            keys, qb[s].reshape(256, HD), (((1,), (1,)), ((), ())), preferred_element_type=F32
        )

    def put_scores(buf, n, s, sub):
        tile = matmul_scores(n, s, sub)
        scores[buf, sub] = tile
        peak[buf, sub] = jnp.max(tile.reshape(64, 8, 256), axis=0)

    def step(n, s, after, after_s):
        buf = s % 2
        across = slice(s * 256, (s + 1) * 256)
        owner, in_flight = n % 2, n // 8
        holder = c + owner - 2 * c * owner
        shown = []
        for sub in range(2):
            span = rank[holder + 2 * sub] <= rank[s]
            cached = 2 * holder + sub < seen[s]
            shown.append(jnp.where(in_flight == 1, span.astype(jnp.int32), cached.astype(jnp.int32)) > 0)
        old = top[:, across]
        new = old
        for sub in range(2):
            most = jnp.max(peak[buf, sub], axis=0, keepdims=True) * SCALE
            new = jnp.maximum(new, jnp.where(shown[sub], most, -FAR))
        fade = jnp.exp2(old - new)
        total = jnp.zeros((HD, 256), F32)
        summed = jnp.zeros((8, 256), F32)
        for sub in range(2):
            put_scores(1 - buf, after, after_s, sub)
            shift = jnp.where(shown[sub], new, FAR)
            weights = jnp.exp2(scores[buf, sub] * SCALE - shift)
            summed = summed + jnp.sum(weights.reshape(64, 8, 256), axis=0)
            across_values = vb[owner, (n % 8) // 2, 2 * (1 - in_flight) + sub].reshape(512, HD).T
            total = total + lax.dot_general(
                across_values, weights.astype(BF), (((1,), (0,)), ((), ())),
                preferred_element_type=F32,
            )
        den[:, across] = den[:, across] * fade + summed
        acc[:, across] = acc[:, across] * fade + total
        top[:, across] = new

    for text in BEFORE:
        event(text)
    for n, (_, dst) in enumerate(small):
        wait_bytes(dst, scalar_sem.at[n])
    acc[...] = jnp.zeros_like(acc)
    den[...] = jnp.zeros_like(den)
    top[...] = jnp.full_like(top, -FAR)
    for sub in range(2):
        put_scores(0, 0, 0, sub)

    def item(n, carry):
        for m, texts in enumerate(DURING):

            @pl.when(n == m)
            def _():
                for text in texts:
                    event(text)

        for s in range(4):
            if s < 3:
                step(n, s, n, s + 1)
            else:
                step(n, s, jnp.minimum(n + 1, 15), 0)
        return carry

    lax.fori_loop(0, 16, item, 0)

    for s in range(4):
        across = slice(s * 256, (s + 1) * 256)
        gain = gate[level[s], head] / jnp.sum(den[:, across], axis=0, keepdims=True)
        att[s] = (acc[:, across] * gain).T.astype(BF).reshape(2, NY, ROWS, HD)
        span = (s + 1) % 4
        parity = (s % 2 + c) % 2
        for half in range(2):
            to = (span // 2) * 4 + 2 * half + parity
            itself = jnp.logical_and(to == z, c == span % 2)
            src = att.at[s, half]
            dst = ret.at[:, :, pl.ds(pl.multiple_of(z * 128, 128), 128)]

            @pl.when(itself)
            def _():
                local_copy(src, dst, back_recv.at[0])

            @pl.when(jnp.logical_not(itself))
            def _():
                remote(src, dst, back_send.at[0], back_recv.at[0], device(x, y, to, span % 2))

    wait_bytes(ret, back_recv.at[0])
    for d in (2, 1, 3, 0):
        to = (y + d) % NY
        src = ret.at[to]
        dst = o_ref.at[0, :, pl.ds(pl.multiple_of(y * 1024, 1024), 1024)]
        if d:
            remote(src, dst, back_send.at[1], back_recv.at[1], device(x, to, z, c))
        else:
            local_copy(src, dst, back_recv.at[1])

    for u in range(QUERY):
        for j in range(4):
            wait_bytes(group(u, j), s_send.at[u, j])
        for j in range(3):
            wait_bytes(group(u, j), x_send.at[u, j])
        n, first, count = UNITS[u]
        if n in (CK, CV):
            for sem in (y_send, z_send):
                wait_bytes(held[n].at[:, pl.ds(first - 2, count), pl.ds(0, 3)], sem.at[u])
        else:
            wait_bytes(held[n].at[pl.ds(0, 3)], y_send.at[u])
            wait_bytes(held[n].at[:, :, pl.ds(0, 896)], z_send.at[u])
    wait_bytes(sq.at[pl.ds(0, 3)], y_send.at[QUERY])

    @pl.when(odd == 0)
    def _():
        wait_bytes(ret.at[:, :, pl.ds(0, 896)], z_send.at[QUERY])
        wait_bytes(ret, back_send.at[0])

    @pl.when(odd == 1)
    def _():
        wait_bytes(ret, z_send.at[QUERY])
        wait_bytes(ret.at[:, :, pl.ds(0, 896)], back_send.at[0])

    wait_bytes(ret.at[pl.ds(0, 3)], back_send.at[1])
    wait_bytes(o_ref, back_recv.at[1])


def local(*operands):
    dma = pltpu.SemaphoreType.DMA
    smem, vmem = pltpu.SMEM, pltpu.VMEM
    everything = (2, NX, 4, 4, NY, ROWS, HD)
    work = 4 * 1024 * 16384 * HD
    return pl.pallas_call(
        kernel,
        out_shape=jax.ShapeDtypeStruct((1, ROWS, HEADS * HD), BF),
        in_specs=[pl.BlockSpec(memory_space=pl.ANY)] * 9,
        out_specs=pl.BlockSpec(memory_space=pltpu.VMEM),
        scratch_shapes=[
            smem((4,), jnp.int32), smem((4,), jnp.int32), smem((4,), jnp.int32), smem((16, 32), F32),
            vmem((4, 2, NY, ROWS, HD), BF), vmem(everything, BF), vmem(everything, BF),
            vmem((NY, 4, 2, ROWS, HD), BF), vmem((NY, ROWS, 1024), BF), vmem((NY, ROWS, 1024), BF),
            vmem((2, 2, NY, ROWS, 256), BF), vmem((2, 2, NY, ROWS, 256), BF),
            vmem((4, 2, NY, ROWS, HD), BF), vmem((NY, ROWS, 1024), BF),
            vmem((2, 2, 512, 256), F32), vmem((2, 2, 8, 256), F32),
            vmem((HD, 1024), F32), vmem((1, 1024), F32), vmem((8, 1024), F32),
            dma((4,)), dma((6,)), dma((6,)), dma((6,)), dma((6,)),
            dma((5, 3)), dma((5, 3)), dma((5, 4)), dma((5, 4)), dma((2,)), dma((2,)),
        ],
        compiler_params=pltpu.CompilerParams(
            collective_id=0, has_side_effects=True, vmem_limit_bytes=56 * 2**20
        ),
        cost_estimate=pl.CostEstimate(
            flops=work, bytes_accessed=16 * 2**20, transcendentals=1024 * 16384
        ),
        name="attend_all",
    )(*operands)


def solution(mesh):
    own, cached = P("slot", "seq", None), P(None, "seq", None)
    placed = (own, own, own, cached, cached, P(), P(), P(), P())
    return jax.shard_map(local, mesh=mesh, in_specs=placed, out_specs=own, check_vma=False)
```

```python
import math

import jax
import jax.numpy as jnp
from jax import lax
from jax.experimental import pallas as pl
from jax.experimental.pallas import tpu as pltpu
from jax.sharding import PartitionSpec as P

HEADS = 32
HD = 128
ROWS = 32
NX, NY, NZ = 4, 4, 8
MESH = pl.DeviceIdType.MESH
BF = jnp.bfloat16
F32 = jnp.float32
FAR = 1e30
SCALE = math.log2(math.e) / math.sqrt(HD)

CK, CV, K, V, Q = range(5)
UNITS = ((CK, 2, 1), (CK, 3, 1), (CV, 2, 2), (K, 0, 2), (V, 0, 2), (Q, 0, 2))
QUERY = 5

BEFORE = ("y0", "y1", "Z0", "Z1", "y2", "y3", "y4", "z0", "z1", "z2", "a0", "Y", "a1", "z3", "a2", "z4", "q")
DURING = (
    ("s00", "s10"),
    ("b0", "b1", "s20"),
    ("b2", "a3", "s01", "s11"),
    ("d0", "d1", "s21"),
    ("d2", "s02", "s12"),
    ("c0", "c1", "a4", "s22"),
    ("c2", "s03", "s13"),
    ("s23",),
    ("s30",),
    ("b3", "s40",),
    ("b4", "s31"),
    ("d3", "s41"),
    ("d4", "s32"),
    ("c3", "s42"),
    ("c4", "s33"),
    ("s43",),
)


def place():
    slot, seq = lax.axis_index("slot"), lax.axis_index("seq")
    return seq // 16, (seq // 4) % 4, (slot // 2) * 4 + seq % 4, slot % 2


def device(x, y, z, core):
    return ((z // 4) * 2 + core, x * 16 + y * 4 + z % 4)


def wait_bytes(ref, sem):
    pltpu.make_async_copy(ref, ref, sem).wait()


def greet(peers):
    barrier = pltpu.get_barrier_semaphore()
    for peer in peers:
        pl.semaphore_signal(barrier, inc=1, device_id=peer, device_id_type=MESH)
    pl.semaphore_wait(barrier, len(peers))


def remote(src, dst, send, recv, peer):
    pltpu.make_async_remote_copy(
        src_ref=src, dst_ref=dst, send_sem=send, recv_sem=recv, device_id=peer, device_id_type=MESH
    ).start()


def local_copy(src, dst, sem):
    pltpu.make_async_copy(src, dst, sem).start()


def kernel(
    q_ref, k_ref, v_ref, ck_ref, cv_ref, rank_ref, level_ref, seen_ref, gate_ref, o_ref,
    rank, level, seen, gate, qb, kb, vb, sq, sk, sv, sck, scv, att,
    scores, peak, acc, top, den,
    scalar_sem, y_send, y_recv, z_send, z_recv, x_send, x_recv, s_send, s_recv,
    back_send, back_recv,
):
    x, y, z, c = place()
    zl, zhi = z % 4, z // 4
    odd = z % 2
    head = y * NZ + z
    q_core = c + odd - 2 * c * odd
    step_x = 1 - 2 * c
    ahead = device((x + step_x + NX) % NX, y, z, c)
    behind = device((x - step_x + NX) % NX, y, z, c)
    other = device(x, y, z, 1 - c)

    small = ((rank_ref, rank), (level_ref, level), (seen_ref, seen), (gate_ref, gate))
    for n, (src, dst) in enumerate(small):
        local_copy(src, dst, scalar_sem.at[n])

    peers = [device(x, (y + d) % NY, z, c) for d in range(1, NY)]
    peers += [device(x, y, (z + d) % NZ, c) for d in range(1, NZ)]
    peers += [device(x, y, (z + d) % NZ, 1 - c) for d in range(NZ)]
    peers += [ahead, behind]
    greet(peers)

    pairs = [((z // 2 + e - c + 4) % 4) for e in range(2)]
    held = {Q: sq, K: sk, V: sv, CK: sck, CV: scv}
    given = {Q: q_ref, K: k_ref, V: v_ref, CK: ck_ref, CV: cv_ref}
    full = {CK: kb, K: kb, CV: vb, V: vb}

    def stage_y(u):
        n, first, count = UNITS[u]
        for d in (1, 2, 3, 0):
            to = (y + d) % NY
            if n in (CK, CV):
                parts = [
                    (
                        given[n].at[
                            pl.ds(2 * c + first - 2, count), :,
                            pl.ds(pl.multiple_of(to * 1024 + pairs[e] * 256, 256), 256),
                        ],
                        held[n].at[e, pl.ds(first - 2, count), y],
                    )
                    for e in range(2)
                ]
            else:
                columns = pl.ds(pl.multiple_of(to * 1024, 1024), 1024)
                parts = [(given[n].at[0, :, columns], held[n].at[y])]
            for src, dst in parts:
                if d:
                    remote(src, dst, y_send.at[u], y_recv.at[u], device(x, to, z, c))
                else:
                    local_copy(src, dst, y_recv.at[u])

    def held_unit(u):
        n, first, count = UNITS[u]
        return held[n].at[:, pl.ds(first - 2, count)] if n in (CK, CV) else held[n]

    def stage_z(u):
        n, first, count = UNITS[u]
        wait_bytes(held_unit(u), y_recv.at[u])
        if n in (CK, CV):
            for e in (0, 1):
                for w in range(2):
                    to = pairs[e] * 2 + w
                    src = held[n].at[e, pl.ds(first - 2, count), :, :, pl.ds(w * 128, 128)]
                    dst = full[n].at[0, 0, pl.ds(first, count), zl]

                    @pl.when(to == z)
                    def _():
                        local_copy(src, dst, z_recv.at[u])

                    @pl.when(to != z)
                    def _():
                        remote(src, dst, z_send.at[u], z_recv.at[u], device(x, y, to, c))

            return
        for d in (4, 3, 5, 2, 6, 1, 7, 0):
            to = (z + d) % NZ
            src = held[n].at[:, :, pl.ds(pl.multiple_of(to * 128, 128), 128)]
            dst = full[n].at[0, 0, zhi, zl]
            if d:
                remote(src, dst, z_send.at[u], z_recv.at[u], device(x, y, to, c))
            else:
                local_copy(src, dst, z_recv.at[u])

    def query_z(part):
        for d in ((4, 3, 5, 2), (6, 1, 7, 0))[part]:
            to = (z + d) % NZ
            for row in range(NY):
                src = q_ref.at[0, :, pl.ds(pl.multiple_of(row * 1024 + to * 128, 128), 128)]
                dst = sq.at[row, zhi * 2 + c, zl // 2]
                if d:
                    remote(src, dst, z_send.at[QUERY], z_recv.at[QUERY], device(x, y, to, q_core))
                else:

                    @pl.when(odd == 0)
                    def _():
                        local_copy(src, dst, z_recv.at[QUERY])

                    @pl.when(odd == 1)
                    def _():
                        remote(src, dst, z_send.at[QUERY], z_recv.at[QUERY], other)

    def query_y():
        wait_bytes(sq, z_recv.at[QUERY])
        for d in (1, 2, 3, 0):
            to = (y + d) % NY
            dst = qb.at[:, :, y]
            if d:
                remote(sq.at[to], dst, y_send.at[QUERY], y_recv.at[QUERY], device(x, to, z, c))
            else:
                local_copy(sq.at[to], dst, y_recv.at[QUERY])

    def group(u, j, owner=0):
        n, first, count = UNITS[u]
        return full[n].at[owner, j, pl.ds(first, count)]

    def share(u, j):
        remote(group(u, j), group(u, j, 1), s_send.at[u, j], s_recv.at[u, j], other)

    def event(text):
        kind = text[0]
        u = int(text[1]) if len(text) > 1 else QUERY
        if kind == "y":
            stage_y(u)
        elif kind == "z":
            stage_z(u)
        elif kind == "Z":
            query_z(u)
        elif kind == "Y":
            query_y()
        elif kind == "q":
            wait_bytes(qb, y_recv.at[QUERY])
        elif kind == "a":
            wait_bytes(group(u, 0), z_recv.at[u])
            remote(group(u, 0), group(u, 1), x_send.at[u, 0], x_recv.at[u, 0], ahead)
            remote(group(u, 0), group(u, 2), x_send.at[u, 1], x_recv.at[u, 1], behind)
            share(u, 0)
        elif kind == "b":
            wait_bytes(group(u, 1), x_recv.at[u, 0])
            remote(group(u, 1), group(u, 3), x_send.at[u, 2], x_recv.at[u, 2], ahead)
            share(u, 1)
        elif kind == "d":
            wait_bytes(group(u, 2), x_recv.at[u, 1])
            share(u, 2)
        elif kind == "c":
            wait_bytes(group(u, 3), x_recv.at[u, 2])
            share(u, 3)
        else:
            j = int(text[2])
            wait_bytes(group(u, j, 1), s_recv.at[u, j])

    def matmul_scores(n, s, sub):
        keys = kb[n % 2, (n % 8) // 2, 2 * (1 - n // 8) + sub].reshape(512, HD)
        return lax.dot_general(
            keys, qb[s].reshape(256, HD), (((1,), (1,)), ((), ())), preferred_element_type=F32
        )

    def put_scores(buf, n, s, sub):
        tile = matmul_scores(n, s, sub)
        scores[buf, sub] = tile
        peak[buf, sub] = jnp.max(tile.reshape(64, 8, 256), axis=0)

    def step(n, s, after, after_s):
        buf = s % 2
        across = slice(s * 256, (s + 1) * 256)
        owner, in_flight = n % 2, n // 8
        holder = c + owner - 2 * c * owner
        shown = []
        for sub in range(2):
            span = rank[holder + 2 * sub] <= rank[s]
            cached = 2 * holder + sub < seen[s]
            shown.append(jnp.where(in_flight == 1, span.astype(jnp.int32), cached.astype(jnp.int32)) > 0)
        old = top[:, across]
        new = old
        for sub in range(2):
            most = jnp.max(peak[buf, sub], axis=0, keepdims=True) * SCALE
            new = jnp.maximum(new, jnp.where(shown[sub], most, -FAR))
        fade = jnp.exp2(old - new)
        total = jnp.zeros((HD, 256), F32)
        summed = jnp.zeros((8, 256), F32)
        for sub in range(2):
            put_scores(1 - buf, after, after_s, sub)
            shift = jnp.where(shown[sub], new, FAR)
            weights = jnp.exp2(scores[buf, sub] * SCALE - shift)
            summed = summed + jnp.sum(weights.reshape(64, 8, 256), axis=0)
            across_values = vb[owner, (n % 8) // 2, 2 * (1 - in_flight) + sub].reshape(512, HD).T
            total = total + lax.dot_general(
                across_values, weights.astype(BF), (((1,), (0,)), ((), ())),
                preferred_element_type=F32,
            )
        den[:, across] = den[:, across] * fade + summed
        acc[:, across] = acc[:, across] * fade + total
        top[:, across] = new

    for text in BEFORE:
        event(text)
    for n, (_, dst) in enumerate(small):
        wait_bytes(dst, scalar_sem.at[n])
    acc[...] = jnp.zeros_like(acc)
    den[...] = jnp.zeros_like(den)
    top[...] = jnp.full_like(top, -FAR)
    for sub in range(2):
        put_scores(0, 0, 0, sub)

    def item(n, carry):
        for m, texts in enumerate(DURING):

            @pl.when(n == m)
            def _():
                for text in texts:
                    event(text)

        for s in range(4):
            if s < 3:
                step(n, s, n, s + 1)
            else:
                step(n, s, jnp.minimum(n + 1, 15), 0)
        return carry

    lax.fori_loop(0, 16, item, 0)

    columns = pl.ds(pl.multiple_of(head * HD, HD), HD)
    for s in range(4):
        across = slice(s * 256, (s + 1) * 256)
        gain = gate[level[s], head] / jnp.sum(den[:, across], axis=0, keepdims=True)
        att[s] = (acc[:, across] * gain).T.astype(BF).reshape(2, NY, ROWS, HD)
        span = (s + 1) % 4
        parity = (s % 2 + c) % 2
        for half in range(2):
            to = (span // 2) * 4 + 2 * half + parity
            itself = jnp.logical_and(to == z, c == span % 2)
            dst = o_ref.at[0, :, columns]
            for d in (2, 1, 3, 0):
                row = (y + d) % NY
                src = att.at[s, half, row]
                if d:
                    remote(src, dst, back_send, back_recv, device(x, row, to, span % 2))
                else:

                    @pl.when(itself)
                    def _():
                        local_copy(src, dst, back_recv)

                    @pl.when(jnp.logical_not(itself))
                    def _():
                        remote(src, dst, back_send, back_recv, device(x, y, to, span % 2))

    for u in range(QUERY):
        for j in range(4):
            wait_bytes(group(u, j), s_send.at[u, j])
        for j in range(3):
            wait_bytes(group(u, j), x_send.at[u, j])
        n, first, count = UNITS[u]
        if n in (CK, CV):
            for sem in (y_send, z_send):
                wait_bytes(held[n].at[:, pl.ds(first - 2, count), pl.ds(0, 3)], sem.at[u])
        else:
            wait_bytes(held[n].at[pl.ds(0, 3)], y_send.at[u])
            wait_bytes(held[n].at[:, :, pl.ds(0, 896)], z_send.at[u])
    wait_bytes(sq.at[pl.ds(0, 3)], y_send.at[QUERY])

    @pl.when(odd == 0)
    def _():
        wait_bytes(sk.at[:, :, pl.ds(0, 896)], z_send.at[QUERY])
        wait_bytes(att, back_send)

    @pl.when(odd == 1)
    def _():
        wait_bytes(sk, z_send.at[QUERY])
        wait_bytes(o_ref.at[:, :, pl.ds(0, 31 * HD)], back_send)

    wait_bytes(o_ref, back_recv)


def local(*operands):
    dma = pltpu.SemaphoreType.DMA
    smem, vmem = pltpu.SMEM, pltpu.VMEM
    everything = (2, NX, 4, 4, NY, ROWS, HD)
    work = 4 * 1024 * 16384 * HD
    return pl.pallas_call(
        kernel,
        out_shape=jax.ShapeDtypeStruct((1, ROWS, HEADS * HD), BF),
        in_specs=[pl.BlockSpec(memory_space=pl.ANY)] * 9,
        out_specs=pl.BlockSpec(memory_space=pltpu.VMEM),
        scratch_shapes=[
            smem((4,), jnp.int32), smem((4,), jnp.int32), smem((4,), jnp.int32), smem((16, 32), F32),
            vmem((4, 2, NY, ROWS, HD), BF), vmem(everything, BF), vmem(everything, BF),
            vmem((NY, 4, 2, ROWS, HD), BF), vmem((NY, ROWS, 1024), BF), vmem((NY, ROWS, 1024), BF),
            vmem((2, 2, NY, ROWS, 256), BF), vmem((2, 2, NY, ROWS, 256), BF),
            vmem((4, 2, NY, ROWS, HD), BF),
            vmem((2, 2, 512, 256), F32), vmem((2, 2, 8, 256), F32),
            vmem((HD, 1024), F32), vmem((1, 1024), F32), vmem((8, 1024), F32),
            dma((4,)), dma((6,)), dma((6,)), dma((6,)), dma((6,)),
            dma((5, 3)), dma((5, 3)), dma((5, 4)), dma((5, 4)), dma, dma,
        ],
        compiler_params=pltpu.CompilerParams(
            collective_id=0, has_side_effects=True, vmem_limit_bytes=56 * 2**20
        ),
        cost_estimate=pl.CostEstimate(
            flops=work, bytes_accessed=16 * 2**20, transcendentals=1024 * 16384
        ),
        name="attend_all",
    )(*operands)


def solution(mesh):
    own, cached = P("slot", "seq", None), P(None, "seq", None)
    placed = (own, own, own, cached, cached, P(), P(), P(), P())
    return jax.shard_map(local, mesh=mesh, in_specs=placed, out_specs=own, check_vma=False)
```

```python
import math

import jax
import jax.numpy as jnp
from jax import lax
from jax.experimental import pallas as pl
from jax.experimental.pallas import tpu as pltpu
from jax.sharding import PartitionSpec as P

HEADS = 32
HD = 128
ROWS = 32
NX, NY, NZ = 4, 4, 8
MESH = pl.DeviceIdType.MESH
BF = jnp.bfloat16
F32 = jnp.float32
FAR = 1e30
SCALE = math.log2(math.e) / math.sqrt(HD)

CK, CV, K, V, Q = range(5)
UNITS = ((CK, 2, 1), (CK, 3, 1), (CV, 2, 2), (K, 0, 2), (V, 0, 2), (Q, 0, 2))
QUERY = 5

BEFORE = (
    "y0", "y1", "Z0", "y2", "y3", "y4", "z0", "Z1", "z1", "z2", "a0", "Y", "a1", "z3", "a2", "z4", "q",
)
DURING = (
    ("s00", "s10"),
    ("b0", "b1", "s20"),
    ("b2", "a3", "s01", "s11"),
    ("d0", "d1", "s21"),
    ("d2", "s02", "s12"),
    ("c0", "c1", "a4", "s22"),
    ("c2", "s03", "s13"),
    ("s23",),
    ("s30",),
    ("b3", "s40",),
    ("b4", "s31"),
    ("d3", "s41"),
    ("d4", "s32"),
    ("c3", "s42"),
    ("c4", "s33"),
    ("s43",),
)


def place():
    slot, seq = lax.axis_index("slot"), lax.axis_index("seq")
    return seq // 16, (seq // 4) % 4, (slot // 2) * 4 + seq % 4, slot % 2


def device(x, y, z, core):
    return ((z // 4) * 2 + core, x * 16 + y * 4 + z % 4)


def wait_bytes(ref, sem):
    pltpu.make_async_copy(ref, ref, sem).wait()


def greet(peers):
    barrier = pltpu.get_barrier_semaphore()
    for peer in peers:
        pl.semaphore_signal(barrier, inc=1, device_id=peer, device_id_type=MESH)
    pl.semaphore_wait(barrier, len(peers))


def remote(src, dst, send, recv, peer):
    pltpu.make_async_remote_copy(
        src_ref=src, dst_ref=dst, send_sem=send, recv_sem=recv, device_id=peer, device_id_type=MESH
    ).start()


def local_copy(src, dst, sem):
    pltpu.make_async_copy(src, dst, sem).start()


def kernel(
    q_ref, k_ref, v_ref, ck_ref, cv_ref, rank_ref, level_ref, seen_ref, gate_ref, o_ref,
    rank, level, seen, gate, qb, kb, vb, sq, sk, sv, sck, scv, att,
    scores, peak, acc, top, den,
    scalar_sem, y_send, y_recv, z_send, z_recv, x_send, x_recv, s_send, s_recv,
    back_send, back_recv,
):
    x, y, z, c = place()
    zl, zhi = z % 4, z // 4
    odd = z % 2
    head = y * NZ + z
    q_core = c + odd - 2 * c * odd
    step_x = 1 - 2 * c
    ahead = device((x + step_x + NX) % NX, y, z, c)
    behind = device((x - step_x + NX) % NX, y, z, c)
    other = device(x, y, z, 1 - c)

    small = ((rank_ref, rank), (level_ref, level), (seen_ref, seen), (gate_ref, gate))
    for n, (src, dst) in enumerate(small):
        local_copy(src, dst, scalar_sem.at[n])

    peers = [device(x, (y + d) % NY, z, c) for d in range(1, NY)]
    peers += [device(x, y, (z + d) % NZ, c) for d in range(1, NZ)]
    peers += [device(x, y, (z + d) % NZ, 1 - c) for d in range(NZ)]
    peers += [ahead, behind]
    greet(peers)

    pairs = [((z // 2 + e - c + 4) % 4) for e in range(2)]
    held = {Q: sq, K: sk, V: sv, CK: sck, CV: scv}
    given = {Q: q_ref, K: k_ref, V: v_ref, CK: ck_ref, CV: cv_ref}
    full = {CK: kb, K: kb, CV: vb, V: vb}

    def stage_y(u):
        n, first, count = UNITS[u]
        for d in (1, 2, 3, 0):
            to = (y + d) % NY
            if n in (CK, CV):
                parts = [
                    (
                        given[n].at[
                            pl.ds(2 * c + first - 2, count), :,
                            pl.ds(pl.multiple_of(to * 1024 + pairs[e] * 256, 256), 256),
                        ],
                        held[n].at[e, pl.ds(first - 2, count), y],
                    )
                    for e in range(2)
                ]
            else:
                columns = pl.ds(pl.multiple_of(to * 1024, 1024), 1024)
                parts = [(given[n].at[0, :, columns], held[n].at[y])]
            for src, dst in parts:
                if d:
                    remote(src, dst, y_send.at[u], y_recv.at[u], device(x, to, z, c))
                else:
                    local_copy(src, dst, y_recv.at[u])

    def held_unit(u):
        n, first, count = UNITS[u]
        return held[n].at[:, pl.ds(first - 2, count)] if n in (CK, CV) else held[n]

    def stage_z(u):
        n, first, count = UNITS[u]
        wait_bytes(held_unit(u), y_recv.at[u])
        if n in (CK, CV):
            for e in (0, 1):
                for w in range(2):
                    to = pairs[e] * 2 + w
                    src = held[n].at[e, pl.ds(first - 2, count), :, :, pl.ds(w * 128, 128)]
                    dst = full[n].at[0, 0, pl.ds(first, count), zl]

                    @pl.when(to == z)
                    def _():
                        local_copy(src, dst, z_recv.at[u])

                    @pl.when(to != z)
                    def _():
                        remote(src, dst, z_send.at[u], z_recv.at[u], device(x, y, to, c))

            return
        for d in (4, 3, 5, 2, 6, 1, 7, 0):
            to = (z + d) % NZ
            src = held[n].at[:, :, pl.ds(pl.multiple_of(to * 128, 128), 128)]
            dst = full[n].at[0, 0, zhi, zl]
            if d:
                remote(src, dst, z_send.at[u], z_recv.at[u], device(x, y, to, c))
            else:
                local_copy(src, dst, z_recv.at[u])

    def query_z(part):
        for d in ((4, 3, 5, 2), (6, 1, 7, 0))[part]:
            to = (z + d) % NZ
            for row in range(NY):
                src = q_ref.at[0, :, pl.ds(pl.multiple_of(row * 1024 + to * 128, 128), 128)]
                dst = sq.at[row, zhi * 2 + c, zl // 2]
                if d:
                    remote(src, dst, z_send.at[QUERY], z_recv.at[QUERY], device(x, y, to, q_core))
                else:

                    @pl.when(odd == 0)
                    def _():
                        local_copy(src, dst, z_recv.at[QUERY])

                    @pl.when(odd == 1)
                    def _():
                        remote(src, dst, z_send.at[QUERY], z_recv.at[QUERY], other)

    def query_y():
        wait_bytes(sq, z_recv.at[QUERY])
        for d in (1, 2, 3, 0):
            to = (y + d) % NY
            dst = qb.at[:, :, y]
            if d:
                remote(sq.at[to], dst, y_send.at[QUERY], y_recv.at[QUERY], device(x, to, z, c))
            else:
                local_copy(sq.at[to], dst, y_recv.at[QUERY])

    def group(u, j, owner=0):
        n, first, count = UNITS[u]
        return full[n].at[owner, j, pl.ds(first, count)]

    def share(u, j):
        remote(group(u, j), group(u, j, 1), s_send.at[u, j], s_recv.at[u, j], other)

    def event(text):
        kind = text[0]
        u = int(text[1]) if len(text) > 1 else QUERY
        if kind == "y":
            stage_y(u)
        elif kind == "z":
            stage_z(u)
        elif kind == "Z":
            query_z(u)
        elif kind == "Y":
            query_y()
        elif kind == "q":
            wait_bytes(qb, y_recv.at[QUERY])
        elif kind == "a":
            wait_bytes(group(u, 0), z_recv.at[u])
            remote(group(u, 0), group(u, 1), x_send.at[u, 0], x_recv.at[u, 0], ahead)
            remote(group(u, 0), group(u, 2), x_send.at[u, 1], x_recv.at[u, 1], behind)
            share(u, 0)
        elif kind == "b":
            wait_bytes(group(u, 1), x_recv.at[u, 0])
            remote(group(u, 1), group(u, 3), x_send.at[u, 2], x_recv.at[u, 2], ahead)
            share(u, 1)
        elif kind == "d":
            wait_bytes(group(u, 2), x_recv.at[u, 1])
            share(u, 2)
        elif kind == "c":
            wait_bytes(group(u, 3), x_recv.at[u, 2])
            share(u, 3)
        else:
            j = int(text[2])
            wait_bytes(group(u, j, 1), s_recv.at[u, j])

    def matmul_scores(n, s, sub):
        keys = kb[n % 2, (n % 8) // 2, 2 * (1 - n // 8) + sub].reshape(512, HD)
        return lax.dot_general(
            keys, qb[s].reshape(256, HD), (((1,), (1,)), ((), ())), preferred_element_type=F32
        )

    def put_scores(buf, n, s, sub):
        tile = matmul_scores(n, s, sub)
        scores[buf, sub] = tile
        peak[buf, sub] = jnp.max(tile.reshape(64, 8, 256), axis=0)

    def step(n, s, after, after_s):
        buf = s % 2
        across = slice(s * 256, (s + 1) * 256)
        owner, in_flight = n % 2, n // 8
        holder = c + owner - 2 * c * owner
        shown = []
        for sub in range(2):
            span = rank[holder + 2 * sub] <= rank[s]
            cached = 2 * holder + sub < seen[s]
            shown.append(jnp.where(in_flight == 1, span.astype(jnp.int32), cached.astype(jnp.int32)) > 0)
        old = top[:, across]
        new = old
        for sub in range(2):
            most = jnp.max(peak[buf, sub], axis=0, keepdims=True) * SCALE
            new = jnp.maximum(new, jnp.where(shown[sub], most, -FAR))
        fade = jnp.exp2(old - new)
        total = jnp.zeros((HD, 256), F32)
        summed = jnp.zeros((8, 256), F32)
        for sub in range(2):
            put_scores(1 - buf, after, after_s, sub)
            shift = jnp.where(shown[sub], new, FAR)
            weights = jnp.exp2(scores[buf, sub] * SCALE - shift)
            summed = summed + jnp.sum(weights.reshape(64, 8, 256), axis=0)
            across_values = vb[owner, (n % 8) // 2, 2 * (1 - in_flight) + sub].reshape(512, HD).T
            total = total + lax.dot_general(
                across_values, weights.astype(BF), (((1,), (0,)), ((), ())),
                preferred_element_type=F32,
            )
        den[:, across] = den[:, across] * fade + summed
        acc[:, across] = acc[:, across] * fade + total
        top[:, across] = new

    for text in BEFORE:
        event(text)
    for n, (_, dst) in enumerate(small):
        wait_bytes(dst, scalar_sem.at[n])
    acc[...] = jnp.zeros_like(acc)
    den[...] = jnp.zeros_like(den)
    top[...] = jnp.full_like(top, -FAR)
    for sub in range(2):
        put_scores(0, 0, 0, sub)

    def item(n, carry):
        for m, texts in enumerate(DURING[:15]):

            @pl.when(n == m)
            def _():
                for text in texts:
                    event(text)

        for s in range(4):
            step(n, s, n + s // 3, (s + 1) % 4)
        return carry

    lax.fori_loop(0, 15, item, 0)
    for text in DURING[15]:
        event(text)

    columns = pl.ds(pl.multiple_of(head * HD, HD), HD)
    for s in range(4):
        step(15, s, 15, min(s + 1, 3))
        across = slice(s * 256, (s + 1) * 256)
        gain = gate[level[s], head] / jnp.sum(den[:, across], axis=0, keepdims=True)
        att[s] = (acc[:, across] * gain).T.astype(BF).reshape(2, NY, ROWS, HD)
        span = (s + 1) % 4
        parity = (s % 2 + c) % 2
        for half in range(2):
            to = (span // 2) * 4 + 2 * half + parity
            itself = jnp.logical_and(to == z, c == span % 2)
            dst = o_ref.at[0, :, columns]
            for d in (2, 1, 3, 0):
                row = (y + d) % NY
                src = att.at[s, half, row]
                if d:
                    remote(src, dst, back_send, back_recv, device(x, row, to, span % 2))
                else:

                    @pl.when(itself)
                    def _():
                        local_copy(src, dst, back_recv)

                    @pl.when(jnp.logical_not(itself))
                    def _():
                        remote(src, dst, back_send, back_recv, device(x, y, to, span % 2))

    for u in range(QUERY):
        for j in range(4):
            wait_bytes(group(u, j), s_send.at[u, j])
        for j in range(3):
            wait_bytes(group(u, j), x_send.at[u, j])
        n, first, count = UNITS[u]
        if n in (CK, CV):
            for sem in (y_send, z_send):
                wait_bytes(held[n].at[:, pl.ds(first - 2, count), pl.ds(0, 3)], sem.at[u])
        else:
            wait_bytes(held[n].at[pl.ds(0, 3)], y_send.at[u])
            wait_bytes(held[n].at[:, :, pl.ds(0, 896)], z_send.at[u])
    wait_bytes(sq.at[pl.ds(0, 3)], y_send.at[QUERY])

    @pl.when(odd == 0)
    def _():
        wait_bytes(sk.at[:, :, pl.ds(0, 896)], z_send.at[QUERY])
        wait_bytes(att, back_send)

    @pl.when(odd == 1)
    def _():
        wait_bytes(sk, z_send.at[QUERY])
        wait_bytes(o_ref.at[:, :, pl.ds(0, 31 * HD)], back_send)

    wait_bytes(o_ref, back_recv)


def local(*operands):
    dma = pltpu.SemaphoreType.DMA
    smem, vmem = pltpu.SMEM, pltpu.VMEM
    everything = (2, NX, 4, 4, NY, ROWS, HD)
    work = 4 * 1024 * 16384 * HD
    return pl.pallas_call(
        kernel,
        out_shape=jax.ShapeDtypeStruct((1, ROWS, HEADS * HD), BF),
        in_specs=[pl.BlockSpec(memory_space=pl.ANY)] * 9,
        out_specs=pl.BlockSpec(memory_space=pl.ANY),
        scratch_shapes=[
            smem((4,), jnp.int32), smem((4,), jnp.int32), smem((4,), jnp.int32), smem((16, 32), F32),
            vmem((4, 2, NY, ROWS, HD), BF), vmem(everything, BF), vmem(everything, BF),
            vmem((NY, 4, 2, ROWS, HD), BF), vmem((NY, ROWS, 1024), BF), vmem((NY, ROWS, 1024), BF),
            vmem((2, 2, NY, ROWS, 256), BF), vmem((2, 2, NY, ROWS, 256), BF),
            vmem((4, 2, NY, ROWS, HD), BF),
            vmem((2, 2, 512, 256), F32), vmem((2, 2, 8, 256), F32),
            vmem((HD, 1024), F32), vmem((1, 1024), F32), vmem((8, 1024), F32),
            dma((4,)), dma((6,)), dma((6,)), dma((6,)), dma((6,)),
            dma((5, 3)), dma((5, 3)), dma((5, 4)), dma((5, 4)), dma, dma,
        ],
        compiler_params=pltpu.CompilerParams(
            collective_id=0, has_side_effects=True, vmem_limit_bytes=56 * 2**20
        ),
        cost_estimate=pl.CostEstimate(
            flops=work, bytes_accessed=16 * 2**20, transcendentals=1024 * 16384
        ),
        name="attend_all",
    )(*operands)


def solution(mesh):
    own, cached = P("slot", "seq", None), P(None, "seq", None)
    placed = (own, own, own, cached, cached, P(), P(), P(), P())
    return jax.shard_map(local, mesh=mesh, in_specs=placed, out_specs=own, check_vma=False)
```

```python
import math

import jax
import jax.numpy as jnp
from jax import lax
from jax.experimental import pallas as pl
from jax.experimental.pallas import tpu as pltpu
from jax.sharding import PartitionSpec as P

HEADS = 32
HD = 128
ROWS = 32
NX, NY, NZ = 4, 4, 8
MESH = pl.DeviceIdType.MESH
BF = jnp.bfloat16
F32 = jnp.float32
FAR = 1e30
SCALE = math.log2(math.e) / math.sqrt(HD)

CK, CV, K, V, Q = range(5)
UNITS = ((CK, 2, 1), (CK, 3, 1), (CV, 2, 2), (K, 0, 2), (V, 0, 2), (Q, 0, 2))
QUERY = 5

BEFORE = (
    "y0", "y1", "Z0", "y2", "y3", "y4", "z0", "Z1", "z1", "z2", "a0", "Y", "a1", "z3", "a2", "z4", "q",
)
DURING = (
    ("s00", "s10"),
    ("b0", "b1", "s20"),
    ("b2", "a3", "s01", "s11"),
    ("d0", "d1", "s21"),
    ("d2", "s02", "s12"),
    ("c0", "c1", "a4", "s22"),
    ("c2", "s03", "s13"),
    ("s23",),
    ("s30",),
    ("b3", "s40",),
    ("b4", "s31"),
    ("d3", "s41"),
    ("d4", "s32"),
    ("c3", "s42"),
    ("c4", "s33"),
    ("s43",),
)


def place():
    slot, seq = lax.axis_index("slot"), lax.axis_index("seq")
    return seq // 16, (seq // 4) % 4, (slot // 2) * 4 + seq % 4, slot % 2


def device(x, y, z, core):
    return ((z // 4) * 2 + core, x * 16 + y * 4 + z % 4)


def wait_bytes(ref, sem):
    pltpu.make_async_copy(ref, ref, sem).wait()


def greet(peers):
    barrier = pltpu.get_barrier_semaphore()
    for peer in peers:
        pl.semaphore_signal(barrier, inc=1, device_id=peer, device_id_type=MESH)
    pl.semaphore_wait(barrier, len(peers))


def remote(src, dst, send, recv, peer):
    pltpu.make_async_remote_copy(
        src_ref=src, dst_ref=dst, send_sem=send, recv_sem=recv, device_id=peer, device_id_type=MESH
    ).start()


def local_copy(src, dst, sem):
    pltpu.make_async_copy(src, dst, sem).start()


def kernel(
    q_ref, k_ref, v_ref, ck_ref, cv_ref, rank_ref, level_ref, seen_ref, gate_ref, o_ref,
    rank, level, seen, gate, qb, kb, vb, sq, sk, sv, sck, scv, att,
    scores, peak, acc, top, den,
    scalar_sem, y_send, y_recv, z_send, z_recv, x_send, x_recv, s_send, s_recv,
    back_send, back_recv,
):
    x, y, z, c = place()
    zl, zhi = z % 4, z // 4
    odd = z % 2
    head = y * NZ + z
    q_core = c + odd - 2 * c * odd
    step_x = 1 - 2 * c
    ahead = device((x + step_x + NX) % NX, y, z, c)
    behind = device((x - step_x + NX) % NX, y, z, c)
    other = device(x, y, z, 1 - c)

    small = ((rank_ref, rank), (level_ref, level), (seen_ref, seen), (gate_ref, gate))
    for n, (src, dst) in enumerate(small):
        local_copy(src, dst, scalar_sem.at[n])

    peers = [device(x, y, (z + d) % NZ, c) for d in (4, 3, 5, 2, 6, 1, 7)]
    peers += [device(x, y, (z + d) % NZ, 1 - c) for d in (4, 3, 5, 2, 6, 1, 7, 0)]
    peers += [device(x, (y + d) % NY, z, c) for d in (2, 1, 3)]
    peers += [ahead, behind]
    greet(peers)

    pairs = [((z // 2 + e - c + 4) % 4) for e in range(2)]
    held = {Q: sq, K: sk, V: sv, CK: sck, CV: scv}
    given = {Q: q_ref, K: k_ref, V: v_ref, CK: ck_ref, CV: cv_ref}
    full = {CK: kb, K: kb, CV: vb, V: vb}

    def stage_y(u):
        n, first, count = UNITS[u]
        for d in (1, 2, 3, 0):
            to = (y + d) % NY
            if n in (CK, CV):
                parts = [
                    (
                        given[n].at[
                            pl.ds(2 * c + first - 2, count), :,
                            pl.ds(pl.multiple_of(to * 1024 + pairs[e] * 256, 256), 256),
                        ],
                        held[n].at[e, pl.ds(first - 2, count), y],
                    )
                    for e in range(2)
                ]
            else:
                columns = pl.ds(pl.multiple_of(to * 1024, 1024), 1024)
                parts = [(given[n].at[0, :, columns], held[n].at[y])]
            for src, dst in parts:
                if d:
                    remote(src, dst, y_send.at[u], y_recv.at[u], device(x, to, z, c))
                else:
                    local_copy(src, dst, y_recv.at[u])

    def held_unit(u):
        n, first, count = UNITS[u]
        return held[n].at[:, pl.ds(first - 2, count)] if n in (CK, CV) else held[n]

    def stage_z(u):
        n, first, count = UNITS[u]
        wait_bytes(held_unit(u), y_recv.at[u])
        if n in (CK, CV):
            for e in (0, 1):
                for w in range(2):
                    to = pairs[e] * 2 + w
                    src = held[n].at[e, pl.ds(first - 2, count), :, :, pl.ds(w * 128, 128)]
                    dst = full[n].at[0, 0, pl.ds(first, count), zl]

                    @pl.when(to == z)
                    def _():
                        local_copy(src, dst, z_recv.at[u])

                    @pl.when(to != z)
                    def _():
                        remote(src, dst, z_send.at[u], z_recv.at[u], device(x, y, to, c))

            return
        for d in (4, 3, 5, 2, 6, 1, 7, 0):
            to = (z + d) % NZ
            src = held[n].at[:, :, pl.ds(pl.multiple_of(to * 128, 128), 128)]
            dst = full[n].at[0, 0, zhi, zl]
            if d:
                remote(src, dst, z_send.at[u], z_recv.at[u], device(x, y, to, c))
            else:
                local_copy(src, dst, z_recv.at[u])

    def query_z(part):
        for d in ((4, 3, 5, 2), (6, 1, 7, 0))[part]:
            to = (z + d) % NZ
            for row in range(NY):
                src = q_ref.at[0, :, pl.ds(pl.multiple_of(row * 1024 + to * 128, 128), 128)]
                dst = sq.at[row, zhi * 2 + c, zl // 2]
                if d:
                    remote(src, dst, z_send.at[QUERY], z_recv.at[QUERY], device(x, y, to, q_core))
                else:

                    @pl.when(odd == 0)
                    def _():
                        local_copy(src, dst, z_recv.at[QUERY])

                    @pl.when(odd == 1)
                    def _():
                        remote(src, dst, z_send.at[QUERY], z_recv.at[QUERY], other)

    def query_y():
        wait_bytes(sq, z_recv.at[QUERY])
        for d in (1, 2, 3, 0):
            to = (y + d) % NY
            dst = qb.at[:, :, y]
            if d:
                remote(sq.at[to], dst, y_send.at[QUERY], y_recv.at[QUERY], device(x, to, z, c))
            else:
                local_copy(sq.at[to], dst, y_recv.at[QUERY])

    def group(u, j, owner=0):
        n, first, count = UNITS[u]
        return full[n].at[owner, j, pl.ds(first, count)]

    def share(u, j):
        remote(group(u, j), group(u, j, 1), s_send.at[u, j], s_recv.at[u, j], other)

    def event(text):
        kind = text[0]
        u = int(text[1]) if len(text) > 1 else QUERY
        if kind == "y":
            stage_y(u)
        elif kind == "z":
            stage_z(u)
        elif kind == "Z":
            query_z(u)
        elif kind == "Y":
            query_y()
        elif kind == "q":
            wait_bytes(qb, y_recv.at[QUERY])
        elif kind == "a":
            wait_bytes(group(u, 0), z_recv.at[u])
            remote(group(u, 0), group(u, 1), x_send.at[u, 0], x_recv.at[u, 0], ahead)
            remote(group(u, 0), group(u, 2), x_send.at[u, 1], x_recv.at[u, 1], behind)
            share(u, 0)
        elif kind == "b":
            wait_bytes(group(u, 1), x_recv.at[u, 0])
            remote(group(u, 1), group(u, 3), x_send.at[u, 2], x_recv.at[u, 2], ahead)
            share(u, 1)
        elif kind == "d":
            wait_bytes(group(u, 2), x_recv.at[u, 1])
            share(u, 2)
        elif kind == "c":
            wait_bytes(group(u, 3), x_recv.at[u, 2])
            share(u, 3)
        else:
            j = int(text[2])
            wait_bytes(group(u, j, 1), s_recv.at[u, j])

    def matmul_scores(n, s, sub):
        keys = kb[n % 2, (n % 8) // 2, 2 * (1 - n // 8) + sub].reshape(512, HD)
        return lax.dot_general(
            keys, qb[s].reshape(256, HD), (((1,), (1,)), ((), ())), preferred_element_type=F32
        )

    def put_scores(buf, n, s, sub):
        tile = matmul_scores(n, s, sub)
        scores[buf, sub] = tile
        peak[buf, sub] = jnp.max(tile.reshape(64, 8, 256), axis=0)

    def step(n, s, after, after_s):
        buf = s % 2
        across = slice(s * 256, (s + 1) * 256)
        owner, in_flight = n % 2, n // 8
        holder = c + owner - 2 * c * owner
        shown = []
        for sub in range(2):
            span = rank[holder + 2 * sub] <= rank[s]
            cached = 2 * holder + sub < seen[s]
            shown.append(jnp.where(in_flight == 1, span.astype(jnp.int32), cached.astype(jnp.int32)) > 0)
        old = top[:, across]
        new = old
        for sub in range(2):
            most = jnp.max(peak[buf, sub], axis=0, keepdims=True) * SCALE
            new = jnp.maximum(new, jnp.where(shown[sub], most, -FAR))
        fade = jnp.exp2(old - new)
        total = jnp.zeros((HD, 256), F32)
        summed = jnp.zeros((8, 256), F32)
        for sub in range(2):
            put_scores(1 - buf, after, after_s, sub)
            shift = jnp.where(shown[sub], new, FAR)
            weights = jnp.exp2(scores[buf, sub] * SCALE - shift)
            summed = summed + jnp.sum(weights.reshape(64, 8, 256), axis=0)
            across_values = vb[owner, (n % 8) // 2, 2 * (1 - in_flight) + sub].reshape(512, HD).T
            total = total + lax.dot_general(
                across_values, weights.astype(BF), (((1,), (0,)), ((), ())),
                preferred_element_type=F32,
            )
        den[:, across] = den[:, across] * fade + summed
        acc[:, across] = acc[:, across] * fade + total
        top[:, across] = new

    for text in BEFORE:
        event(text)
    for n, (_, dst) in enumerate(small):
        wait_bytes(dst, scalar_sem.at[n])
    acc[...] = jnp.zeros_like(acc)
    den[...] = jnp.zeros_like(den)
    top[...] = jnp.full_like(top, -FAR)
    for sub in range(2):
        put_scores(0, 0, 0, sub)

    def item(n, carry):
        for m, texts in enumerate(DURING[:15]):

            @pl.when(n == m)
            def _():
                for text in texts:
                    event(text)

        for s in range(4):
            step(n, s, n + s // 3, (s + 1) % 4)
        return carry

    lax.fori_loop(0, 15, item, 0)
    for text in DURING[15]:
        event(text)

    columns = pl.ds(pl.multiple_of(head * HD, HD), HD)
    for s in range(4):
        step(15, s, 15, min(s + 1, 3))
        across = slice(s * 256, (s + 1) * 256)
        gain = gate[level[s], head] / jnp.sum(den[:, across], axis=0, keepdims=True)
        att[s] = (acc[:, across] * gain).T.astype(BF).reshape(2, NY, ROWS, HD)
        span = (s + 1) % 4
        parity = (s % 2 + c) % 2
        for half in range(2):
            to = (span // 2) * 4 + 2 * half + parity
            itself = jnp.logical_and(to == z, c == span % 2)
            dst = o_ref.at[head]
            for d in (2, 1, 3, 0):
                row = (y + d) % NY
                src = att.at[s, half, row]
                if d:
                    remote(src, dst, back_send, back_recv, device(x, row, to, span % 2))
                else:

                    @pl.when(itself)
                    def _():
                        local_copy(src, dst, back_recv)

                    @pl.when(jnp.logical_not(itself))
                    def _():
                        remote(src, dst, back_send, back_recv, device(x, y, to, span % 2))

    for u in range(QUERY):
        for j in range(4):
            wait_bytes(group(u, j), s_send.at[u, j])
        for j in range(3):
            wait_bytes(group(u, j), x_send.at[u, j])
        n, first, count = UNITS[u]
        if n in (CK, CV):
            for sem in (y_send, z_send):
                wait_bytes(held[n].at[:, pl.ds(first - 2, count), pl.ds(0, 3)], sem.at[u])
        else:
            wait_bytes(held[n].at[pl.ds(0, 3)], y_send.at[u])
            wait_bytes(held[n].at[:, :, pl.ds(0, 896)], z_send.at[u])
    wait_bytes(sq.at[pl.ds(0, 3)], y_send.at[QUERY])

    @pl.when(odd == 0)
    def _():
        wait_bytes(sk.at[:, :, pl.ds(0, 896)], z_send.at[QUERY])
        wait_bytes(att, back_send)

    @pl.when(odd == 1)
    def _():
        wait_bytes(sk, z_send.at[QUERY])
        wait_bytes(o_ref.at[pl.ds(0, 31)], back_send)

    wait_bytes(o_ref, back_recv)


def local(*operands):
    dma = pltpu.SemaphoreType.DMA
    smem, vmem = pltpu.SMEM, pltpu.VMEM
    everything = (2, NX, 4, 4, NY, ROWS, HD)
    work = 4 * 1024 * 16384 * HD
    heads = pl.pallas_call(
        kernel,
        out_shape=jax.ShapeDtypeStruct((HEADS, ROWS, HD), BF),
        in_specs=[pl.BlockSpec(memory_space=pl.ANY)] * 9,
        out_specs=pl.BlockSpec(memory_space=pl.ANY),
        scratch_shapes=[
            smem((4,), jnp.int32), smem((4,), jnp.int32), smem((4,), jnp.int32), smem((16, 32), F32),
            vmem((4, 2, NY, ROWS, HD), BF), vmem(everything, BF), vmem(everything, BF),
            vmem((NY, 4, 2, ROWS, HD), BF), vmem((NY, ROWS, 1024), BF), vmem((NY, ROWS, 1024), BF),
            vmem((2, 2, NY, ROWS, 256), BF), vmem((2, 2, NY, ROWS, 256), BF),
            vmem((4, 2, NY, ROWS, HD), BF),
            vmem((2, 2, 512, 256), F32), vmem((2, 2, 8, 256), F32),
            vmem((HD, 1024), F32), vmem((1, 1024), F32), vmem((8, 1024), F32),
            dma((4,)), dma((6,)), dma((6,)), dma((6,)), dma((6,)),
            dma((5, 3)), dma((5, 3)), dma((5, 4)), dma((5, 4)), dma, dma,
        ],
        compiler_params=pltpu.CompilerParams(
            collective_id=0, has_side_effects=True, vmem_limit_bytes=56 * 2**20
        ),
        cost_estimate=pl.CostEstimate(
            flops=work, bytes_accessed=16 * 2**20, transcendentals=1024 * 16384
        ),
        name="attend_all",
    )(*operands)
    return heads.transpose(1, 0, 2).reshape(1, ROWS, HEADS * HD)


def solution(mesh):
    own, cached = P("slot", "seq", None), P(None, "seq", None)
    placed = (own, own, own, cached, cached, P(), P(), P(), P())
    return jax.shard_map(local, mesh=mesh, in_specs=placed, out_specs=own, check_vma=False)
```

```python
import math

import jax
import jax.numpy as jnp
from jax import lax
from jax.experimental import pallas as pl
from jax.experimental.pallas import tpu as pltpu
from jax.sharding import PartitionSpec as P

HEADS = 32
HD = 128
ROWS = 32
NX, NY, NZ = 4, 4, 8
MESH = pl.DeviceIdType.MESH
BF = jnp.bfloat16
F32 = jnp.float32
FAR = 1e30
SCALE = math.log2(math.e) / math.sqrt(HD)

CK, CV, K, V, Q = range(5)
UNITS = ((CK, 2, 1), (CK, 3, 1), (CV, 2, 2), (K, 0, 2), (V, 0, 2), (Q, 0, 2))
QUERY = 5

BEFORE = (
    "y0", "y1", "Z0", "y2", "y3", "y4", "z0", "Z1", "z1", "z2", "a0", "Y", "a1", "z3", "a2", "z4", "q",
)
DURING = (
    ("s00", "s10"),
    ("b0", "b1", "s20"),
    ("b2", "a3", "s01", "s11"),
    ("d0", "d1", "s21"),
    ("d2", "s02", "s12"),
    ("c0", "c1", "a4", "s22"),
    ("c2", "s03", "s13"),
    ("s23",),
    ("s30",),
    ("b3", "s40",),
    ("b4", "s31"),
    ("d3", "s41"),
    ("d4", "s32"),
    ("c3", "s42"),
    ("c4", "s33"),
    ("s43",),
)


def place():
    slot, seq = lax.axis_index("slot"), lax.axis_index("seq")
    return seq // 16, (seq // 4) % 4, (slot // 2) * 4 + seq % 4, slot % 2


def device(x, y, z, core):
    return ((z // 4) * 2 + core, x * 16 + y * 4 + z % 4)


def wait_bytes(ref, sem):
    pltpu.make_async_copy(ref, ref, sem).wait()


def greet(peers):
    barrier = pltpu.get_barrier_semaphore()
    for peer in peers:
        pl.semaphore_signal(barrier, inc=1, device_id=peer, device_id_type=MESH)
    pl.semaphore_wait(barrier, len(peers))


def remote(src, dst, send, recv, peer):
    pltpu.make_async_remote_copy(
        src_ref=src, dst_ref=dst, send_sem=send, recv_sem=recv, device_id=peer, device_id_type=MESH
    ).start()


def local_copy(src, dst, sem):
    pltpu.make_async_copy(src, dst, sem).start()


def kernel(
    q_ref, k_ref, v_ref, ck_ref, cv_ref, rank_ref, level_ref, seen_ref, gate_ref, o_ref,
    rank, level, seen, gate, qb, kb, vb, sq, sk, sv, sck, scv, att,
    scores, peak, acc, top, den,
    scalar_sem, y_send, y_recv, z_send, z_recv, x_send, x_recv, s_send, s_recv,
    back_send, back_recv,
):
    x, y, z, c = place()
    zl, zhi = z % 4, z // 4
    odd = z % 2
    head = y * NZ + z
    q_core = c + odd - 2 * c * odd
    step_x = 1 - 2 * c
    ahead = device((x + step_x + NX) % NX, y, z, c)
    behind = device((x - step_x + NX) % NX, y, z, c)
    other = device(x, y, z, 1 - c)

    small = ((rank_ref, rank), (level_ref, level), (seen_ref, seen), (gate_ref, gate))
    for n, (src, dst) in enumerate(small):
        local_copy(src, dst, scalar_sem.at[n])

    peers = [device(x, y, (z + d) % NZ, c) for d in (4, 3, 5, 2, 6, 1, 7)]
    peers += [device(x, y, (z + d) % NZ, 1 - c) for d in (4, 3, 5, 2, 6, 1, 7, 0)]
    peers += [device(x, (y + d) % NY, z, c) for d in (2, 1, 3)]
    peers += [ahead, behind]
    greet(peers)

    pairs = [((z // 2 + e - c + 4) % 4) for e in range(2)]
    held = {Q: sq, K: sk, V: sv, CK: sck, CV: scv}
    given = {Q: q_ref, K: k_ref, V: v_ref, CK: ck_ref, CV: cv_ref}
    full = {CK: kb, K: kb, CV: vb, V: vb}

    def stage_y(u):
        n, first, count = UNITS[u]
        for d in (1, 2, 3, 0):
            to = (y + d) % NY
            if n in (CK, CV):
                parts = [
                    (
                        given[n].at[
                            pl.ds(2 * c + first - 2, count), :,
                            pl.ds(pl.multiple_of(to * 1024 + pairs[e] * 256, 256), 256),
                        ],
                        held[n].at[e, pl.ds(first - 2, count), y],
                    )
                    for e in range(2)
                ]
            else:
                columns = pl.ds(pl.multiple_of(to * 1024, 1024), 1024)
                parts = [(given[n].at[0, :, columns], held[n].at[y])]
            for src, dst in parts:
                if d:
                    remote(src, dst, y_send.at[u], y_recv.at[u], device(x, to, z, c))
                else:
                    local_copy(src, dst, y_recv.at[u])

    def held_unit(u):
        n, first, count = UNITS[u]
        return held[n].at[:, pl.ds(first - 2, count)] if n in (CK, CV) else held[n]

    def stage_z(u):
        n, first, count = UNITS[u]
        wait_bytes(held_unit(u), y_recv.at[u])
        if n in (CK, CV):
            for e in (0, 1):
                for w in range(2):
                    to = pairs[e] * 2 + w
                    src = held[n].at[e, pl.ds(first - 2, count), :, :, pl.ds(w * 128, 128)]
                    dst = full[n].at[0, 0, pl.ds(first, count), zl]

                    @pl.when(to == z)
                    def _():
                        local_copy(src, dst, z_recv.at[u])

                    @pl.when(to != z)
                    def _():
                        remote(src, dst, z_send.at[u], z_recv.at[u], device(x, y, to, c))

            return
        for d in (4, 3, 5, 2, 6, 1, 7, 0):
            to = (z + d) % NZ
            src = held[n].at[:, :, pl.ds(pl.multiple_of(to * 128, 128), 128)]
            dst = full[n].at[0, 0, zhi, zl]
            if d:
                remote(src, dst, z_send.at[u], z_recv.at[u], device(x, y, to, c))
            else:
                local_copy(src, dst, z_recv.at[u])

    def query_z(part):
        for d in ((4, 3, 5, 2), (6, 1, 7, 0))[part]:
            to = (z + d) % NZ
            for row in range(NY):
                src = q_ref.at[0, :, pl.ds(pl.multiple_of(row * 1024 + to * 128, 128), 128)]
                dst = sq.at[row, zhi * 2 + c, zl // 2]
                if d:
                    remote(src, dst, z_send.at[QUERY], z_recv.at[QUERY], device(x, y, to, q_core))
                else:

                    @pl.when(odd == 0)
                    def _():
                        local_copy(src, dst, z_recv.at[QUERY])

                    @pl.when(odd == 1)
                    def _():
                        remote(src, dst, z_send.at[QUERY], z_recv.at[QUERY], other)

    def query_y():
        wait_bytes(sq, z_recv.at[QUERY])
        for d in (1, 2, 3, 0):
            to = (y + d) % NY
            dst = qb.at[:, :, y]
            if d:
                remote(sq.at[to], dst, y_send.at[QUERY], y_recv.at[QUERY], device(x, to, z, c))
            else:
                local_copy(sq.at[to], dst, y_recv.at[QUERY])

    def group(u, j, owner=0):
        n, first, count = UNITS[u]
        return full[n].at[owner, j, pl.ds(first, count)]

    def share(u, j):
        remote(group(u, j), group(u, j, 1), s_send.at[u, j], s_recv.at[u, j], other)

    def event(text):
        kind = text[0]
        u = int(text[1]) if len(text) > 1 else QUERY
        if kind == "y":
            stage_y(u)
        elif kind == "z":
            stage_z(u)
        elif kind == "Z":
            query_z(u)
        elif kind == "Y":
            query_y()
        elif kind == "q":
            wait_bytes(qb, y_recv.at[QUERY])
        elif kind == "a":
            wait_bytes(group(u, 0), z_recv.at[u])
            remote(group(u, 0), group(u, 1), x_send.at[u, 0], x_recv.at[u, 0], ahead)
            remote(group(u, 0), group(u, 2), x_send.at[u, 1], x_recv.at[u, 1], behind)
            share(u, 0)
        elif kind == "b":
            wait_bytes(group(u, 1), x_recv.at[u, 0])
            remote(group(u, 1), group(u, 3), x_send.at[u, 2], x_recv.at[u, 2], ahead)
            share(u, 1)
        elif kind == "d":
            wait_bytes(group(u, 2), x_recv.at[u, 1])
            share(u, 2)
        elif kind == "c":
            wait_bytes(group(u, 3), x_recv.at[u, 2])
            share(u, 3)
        else:
            j = int(text[2])
            wait_bytes(group(u, j, 1), s_recv.at[u, j])

    def matmul_scores(n, s, sub):
        keys = kb[n % 2, (n % 8) // 2, 2 * (1 - n // 8) + sub].reshape(512, HD)
        return lax.dot_general(
            keys, qb[s].reshape(256, HD), (((1,), (1,)), ((), ())), preferred_element_type=F32
        )

    def put_scores(buf, n, s, sub):
        tile = matmul_scores(n, s, sub)
        scores[buf, sub] = tile
        peak[buf, sub] = jnp.max(tile.reshape(64, 8, 256), axis=0)

    def step(n, s, after, after_s):
        buf = s % 2
        across = slice(s * 256, (s + 1) * 256)
        owner, in_flight = n % 2, n // 8
        holder = c + owner - 2 * c * owner
        shown = []
        for sub in range(2):
            span = rank[holder + 2 * sub] <= rank[s]
            cached = 2 * holder + sub < seen[s]
            shown.append(jnp.where(in_flight == 1, span.astype(jnp.int32), cached.astype(jnp.int32)) > 0)
        old = top[:, across]
        new = old
        for sub in range(2):
            most = jnp.max(peak[buf, sub], axis=0, keepdims=True) * SCALE
            new = jnp.maximum(new, jnp.where(shown[sub], most, -FAR))
        fade = jnp.exp2(old - new)
        total = jnp.zeros((HD, 256), F32)
        summed = jnp.zeros((8, 256), F32)
        for sub in range(2):
            if after is not None:
                put_scores(1 - buf, after, after_s, sub)
            shift = jnp.where(shown[sub], new, FAR)
            weights = jnp.exp2(scores[buf, sub] * SCALE - shift)
            summed = summed + jnp.sum(weights.reshape(64, 8, 256), axis=0)
            across_values = vb[owner, (n % 8) // 2, 2 * (1 - in_flight) + sub].reshape(512, HD).T
            total = total + lax.dot_general(
                across_values, weights.astype(BF), (((1,), (0,)), ((), ())),
                preferred_element_type=F32,
            )
        den[:, across] = den[:, across] * fade + summed
        acc[:, across] = acc[:, across] * fade + total
        top[:, across] = new

    for text in BEFORE:
        event(text)
    for n, (_, dst) in enumerate(small):
        wait_bytes(dst, scalar_sem.at[n])
    acc[...] = jnp.zeros_like(acc)
    den[...] = jnp.zeros_like(den)
    top[...] = jnp.full_like(top, -FAR)
    for sub in range(2):
        put_scores(0, 0, 0, sub)

    def item(n, carry):
        for m, texts in enumerate(DURING[:15]):

            @pl.when(n == m)
            def _():
                for text in texts:
                    event(text)

        for s in range(4):
            step(n, s, n + s // 3, (s + 1) % 4)
        return carry

    lax.fori_loop(0, 15, item, 0)
    for text in DURING[15]:
        event(text)

    columns = pl.ds(pl.multiple_of(head * HD, HD), HD)
    for s in range(4):
        step(15, s, 15 if s < 3 else None, s + 1)
        across = slice(s * 256, (s + 1) * 256)
        gain = gate[level[s], head] / jnp.sum(den[:, across], axis=0, keepdims=True)
        att[s] = (acc[:, across] * gain).T.astype(BF).reshape(2, NY, ROWS, HD)
        span = (s + 1) % 4
        parity = (s % 2 + c) % 2
        for half in range(2):
            to = (span // 2) * 4 + 2 * half + parity
            itself = jnp.logical_and(to == z, c == span % 2)
            dst = o_ref.at[head]
            for d in (2, 1, 3, 0):
                row = (y + d) % NY
                src = att.at[s, half, row]
                if d:
                    remote(src, dst, back_send, back_recv, device(x, row, to, span % 2))
                else:

                    @pl.when(itself)
                    def _():
                        local_copy(src, dst, back_recv)

                    @pl.when(jnp.logical_not(itself))
                    def _():
                        remote(src, dst, back_send, back_recv, device(x, y, to, span % 2))

    for u in range(QUERY):
        for j in range(4):
            wait_bytes(group(u, j), s_send.at[u, j])
        for j in range(3):
            wait_bytes(group(u, j), x_send.at[u, j])
        n, first, count = UNITS[u]
        if n in (CK, CV):
            for sem in (y_send, z_send):
                wait_bytes(held[n].at[:, pl.ds(first - 2, count), pl.ds(0, 3)], sem.at[u])
        else:
            wait_bytes(held[n].at[pl.ds(0, 3)], y_send.at[u])
            wait_bytes(held[n].at[:, :, pl.ds(0, 896)], z_send.at[u])
    wait_bytes(sq.at[pl.ds(0, 3)], y_send.at[QUERY])

    @pl.when(odd == 0)
    def _():
        wait_bytes(sk.at[:, :, pl.ds(0, 896)], z_send.at[QUERY])
        wait_bytes(att, back_send)

    @pl.when(odd == 1)
    def _():
        wait_bytes(sk, z_send.at[QUERY])
        wait_bytes(o_ref.at[pl.ds(0, 31)], back_send)

    wait_bytes(o_ref, back_recv)


def local(*operands):
    dma = pltpu.SemaphoreType.DMA
    smem, vmem = pltpu.SMEM, pltpu.VMEM
    everything = (2, NX, 4, 4, NY, ROWS, HD)
    work = 4 * 1024 * 16384 * HD
    heads = pl.pallas_call(
        kernel,
        out_shape=jax.ShapeDtypeStruct((HEADS, ROWS, HD), BF),
        in_specs=[pl.BlockSpec(memory_space=pl.ANY)] * 9,
        out_specs=pl.BlockSpec(memory_space=pl.ANY),
        scratch_shapes=[
            smem((4,), jnp.int32), smem((4,), jnp.int32), smem((4,), jnp.int32), smem((16, 32), F32),
            vmem((4, 2, NY, ROWS, HD), BF), vmem(everything, BF), vmem(everything, BF),
            vmem((NY, 4, 2, ROWS, HD), BF), vmem((NY, ROWS, 1024), BF), vmem((NY, ROWS, 1024), BF),
            vmem((2, 2, NY, ROWS, 256), BF), vmem((2, 2, NY, ROWS, 256), BF),
            vmem((4, 2, NY, ROWS, HD), BF),
            vmem((2, 2, 512, 256), F32), vmem((2, 2, 8, 256), F32),
            vmem((HD, 1024), F32), vmem((1, 1024), F32), vmem((8, 1024), F32),
            dma((4,)), dma((6,)), dma((6,)), dma((6,)), dma((6,)),
            dma((5, 3)), dma((5, 3)), dma((5, 4)), dma((5, 4)), dma, dma,
        ],
        compiler_params=pltpu.CompilerParams(
            collective_id=0, has_side_effects=True, vmem_limit_bytes=56 * 2**20
        ),
        cost_estimate=pl.CostEstimate(
            flops=work, bytes_accessed=16 * 2**20, transcendentals=1024 * 16384
        ),
        name="attend_all",
    )(*operands)
    return heads.transpose(1, 0, 2).reshape(1, ROWS, HEADS * HD)


def solution(mesh):
    own, cached = P("slot", "seq", None), P(None, "seq", None)
    placed = (own, own, own, cached, cached, P(), P(), P(), P())
    return jax.shard_map(local, mesh=mesh, in_specs=placed, out_specs=own, check_vma=False)
```
